256 devices in a mesh: gx: 16 (over y, z_hi), gy: 4 (over x), gz: 4 (over z_lo, core).
Axes of the slice: x: 4, y: 4, z: 8 (z_hi: 4, z_lo: 2; z = z_hi * 2 + z_lo), core: 2. Of those that a mesh axis runs over, the one named last changes fastest.
Arguments:
- fine: bfloat16 [256, 128, 32, 128], P('gx', 'gy', 'gz'), may hold values from -6 to 6
- occupied: int32 [16, 8, 4], P('gx', 'gy', 'gz'), may hold values 0 or 1
- w_down: bfloat16 [4, 128, 128], replicated, may hold values from -0.25 to 0.25
- w_conv: bfloat16 [27, 128, 128], replicated, may hold values from -0.109375 to 0.109375
- cotangent: bfloat16 [128, 64, 32, 128], P('gx', 'gy', 'gz'), may hold values from -6 to 6
Outputs:
- section_out: bfloat16 [128, 64, 32, 128], P('gx', 'gy', 'gz')
- d_fine: bfloat16 [256, 128, 32, 128], P('gx', 'gy', 'gz')
- d_wconv: float32 [27, 128, 128], P(None, 'gx')
- d_wdown: float32 [4, 128, 128], P(None, 'gx')
The draws below stay inside these ranges and needn't reach their ends.
All inputs are finite; a program needn't handle non-finite values. No bound on the sum of `occupied` on one device may be relied on, other than what follows from the above.
Results may differ from the reference program's by a relative error of at most 0.013.
Values may be sent and summed in bfloat16 or wider, within the bound.
A program may use at most 64 MiB of HBM per device.

```python
import jax
import jax.numpy as jnp
from jax import lax

C_IN = 64
C_OUT = 128
BRICK = 8
MX = 16
MY = 8
MZ = 4
NX = 128
NY = 64
NZ = 32


def place_ends(entries, key, least, top_value):
    longest = entries.shape.index(max(entries.shape))
    spots = []
    for shift in (0, 1):
        where = [jax.random.randint(jax.random.fold_in(key, axis), (), 0, length) for axis, length in enumerate(entries.shape)]
        where[longest] = (where[longest] + shift) % entries.shape[longest]
        spots.append(tuple(where))
    return entries.at[spots[0]].set(least).at[spots[1]].set(top_value)


def block_levels(stream_key, extent, shards, low, largest):
    def one(dim, parts):
        heights = jax.random.uniform(jax.random.fold_in(jax.random.fold_in(stream_key, 6), dim), (parts,), jnp.float32, low / len(shards), largest / len(shards))
        return jnp.repeat(jnp.exp(heights), extent[dim] // parts).reshape((-1,) + (1,) * (len(extent) - dim - 1))

    gain = one(*shards[0])
    for cut in shards[1:]:
        gain = gain * one(*cut)
    return gain


def scatter_about(rng, dims, scale, reach, shards=(), dtype=jnp.bfloat16):
    loudness = block_levels(rng, dims, shards, -0.22, 0.18) if shards else 1.0
    values = jax.random.normal(rng, dims, jnp.float32) * scale * loudness
    return jnp.minimum(jnp.maximum(values, -reach), reach).astype(dtype)


def setup_inputs(seed: int = 0) -> dict:
    key_list = jax.random.split(jax.random.key(seed), 6)
    fine = scatter_about(key_list[0], (2 * NX, 2 * NY, NZ, 2 * C_IN), 1.0, 6.0, ((0, 16), (1, 4), (2, 4)))
    occupied = place_ends((jax.random.randint(key_list[1], (MX, MY, MZ), 0, 4) < 1).astype(jnp.int32), jax.random.fold_in(key_list[1], 1), 0, 1)
    w_down = scatter_about(key_list[2], (4, 2 * C_IN, C_OUT), (8 * C_IN) ** -0.5, 0.25)
    w_conv = scatter_about(key_list[3], (27, C_OUT, C_OUT), (27 * C_OUT) ** -0.5, 0.109375)
    cotangent = scatter_about(key_list[4], (NX, NY, NZ, C_OUT), 1.0, 6.0, ((0, 16), (1, 4), (2, 4)))
    return dict(fine=fine, occupied=occupied, w_down=w_down, w_conv=w_conv, cotangent=cotangent)


def expand_mask(occupied):
    cells = occupied.astype(jnp.float32)
    cells = jnp.repeat(cells, BRICK, axis=0)
    cells = jnp.repeat(cells, BRICK, axis=1)
    cells = jnp.repeat(cells, BRICK, axis=2)
    return cells[..., None]


def patches(fine):
    sizex = fine.shape[0] // 2
    sizey = fine.shape[1] // 2
    split = fine.reshape(sizex, 2, sizey, 2, fine.shape[2], fine.shape[3])
    return [split[:, a, :, b] for a in range(2) for b in range(2)]


def reference(fine, occupied, w_down, w_conv, cotangent):
    occ = expand_mask(occupied)
    sizex, sizey, sizez, width = cotangent.shape
    cells = sizex * sizey * sizez
    pieces = patches(fine)
    down = jnp.zeros((cells, width), jnp.float32)
    for index in range(4):
        down = down + jnp.dot(pieces[index].reshape(cells, -1), w_down[index], preferred_element_type=jnp.float32)
    z_val = (occ * down.reshape(sizex, sizey, sizez, width)).astype(jnp.bfloat16)
    act = jnp.maximum(z_val, jnp.zeros((), jnp.bfloat16))
    masked = (occ * cotangent.astype(jnp.float32)).astype(jnp.bfloat16)
    act_pad = jnp.pad(act, ((1, 1), (1, 1), (1, 1), (0, 0)))
    grad_pad = jnp.pad(masked, ((1, 1), (1, 1), (1, 1), (0, 0)))
    masked_flat = masked.reshape(cells, width)
    forward = jnp.zeros((cells, width), jnp.float32)
    backward = jnp.zeros((cells, width), jnp.float32)
    grads = []
    for dx in range(3):
        for dy in range(3):
            for dz in range(3):
                tap = 9 * dx + 3 * dy + dz
                ahead = act_pad[dx:dx + sizex, dy:dy + sizey, dz:dz + sizez].reshape(cells, width)
                behind = grad_pad[2 - dx:2 - dx + sizex, 2 - dy:2 - dy + sizey, 2 - dz:2 - dz + sizez].reshape(cells, width)
                forward = forward + jnp.dot(ahead, w_conv[tap], preferred_element_type=jnp.float32)
                backward = backward + lax.dot_general(behind, w_conv[tap], (((1,), (1,)), ((), ())), preferred_element_type=jnp.float32)
                grads.append(lax.dot_general(ahead, masked_flat, (((0,), (0,)), ((), ())), preferred_element_type=jnp.float32))
    scale = float(NX * NY * NZ) ** -0.5
    forward = forward.reshape(sizex, sizey, sizez, width)
    backward = backward.reshape(sizex, sizey, sizez, width)
    section_out = (z_val.astype(jnp.float32) + occ * forward).astype(jnp.bfloat16)
    d_wconv = jnp.stack(grads) * scale
    positive = z_val > 0
    dz_val = (occ * (cotangent.astype(jnp.float32) + jnp.where(positive, backward, 0.0))).astype(jnp.bfloat16)
    dz_flat = dz_val.reshape(cells, width)
    down_grads = []
    outputs = []
    for index in range(4):
        down_grads.append(lax.dot_general(pieces[index].reshape(cells, -1), dz_flat, (((0,), (0,)), ((), ())), preferred_element_type=jnp.float32))
        outputs.append(lax.dot_general(dz_flat, w_down[index], (((1,), (1,)), ((), ())), preferred_element_type=jnp.float32).astype(jnp.bfloat16))
    d_wdown = jnp.stack(down_grads) * scale
    stacked = jnp.stack(outputs).reshape(2, 2, sizex, sizey, sizez, -1)
    d_fine = jnp.transpose(stacked, (2, 0, 3, 1, 4, 5)).reshape(2 * sizex, 2 * sizey, sizez, -1)
    return section_out, d_fine, d_wconv, d_wdown
```

```python
import jax
import jax.numpy as jnp
from jax import lax
from jax.experimental import pallas as pl
from jax.experimental.pallas import tpu as pltpu
from jax.sharding import PartitionSpec as P

BF = jnp.bfloat16
F32 = jnp.float32
MESH = pl.DeviceIdType.MESH

NGX, NGY, NGZ = 16, 4, 4
NEIGHBOURS = [
    (sx, sy, sz)
    for sz in (-1, 1, 0)
    for sy in (-1, 0, 1)
    for sx in (-1, 0, 1)
    if (sx, sy, sz) != (0, 0, 0)
]
GROUPS = [3, 4, 5, 0, 1, 2, 6, 7, 8]
SLOTS = [3 * g + 2 - b for g in GROUPS for b in range(3)] + [27, 28, 29, 30]


def dot(a, b, ca, cb):
    return lax.dot_general(a, b, (((ca,), (cb,)), ((), ())), preferred_element_type=F32)


def kernel(
    fine, occupied, w_down, w_conv, cot,
    out, d_fine, d_wconv, d_wdown,
    fine_v, wd_v, wc_v, cot_v,
    mp, ap, mz, az, mzr, azr, me_v, mo_v, ae_v, ao_v,
    zv, act_t, patch_t, acc, dz_v, grads,
    r0, p1, r1, s1acc, p2, r3, p3, r4,
    load_sem, mh_s, mh_r, ah_s, ah_r,
    s0_s, s0_r, s1_s, s1_r, s3_s, s3_r, s4_s, s4_r,
):
    gx, gy, gz = lax.axis_index("gx"), lax.axis_index("gy"), lax.axis_index("gz")
    yy, zhi, xx = gx // 4, lax.rem(gx, 4), gy
    zlo, core = gz // 2, lax.rem(gz, 2)
    zz = zhi * 2 + zlo

    def near(s):
        return (
            lax.rem(gx + s[0] + NGX, NGX),
            lax.rem(gy + s[1] + NGY, NGY),
            lax.rem(gz + s[2] + NGZ, NGZ),
        )

    other = (gx, gy, gz + 1 - 2 * core)

    def plane(n):
        tx, ty = lax.rem(xx + lax.rem(n, 4), 4), lax.rem(yy + n // 4, 4)
        return tx, ty, (ty * 4 + zhi, tx, gz)

    def column(n):
        tz = lax.rem(zz + n, 8)
        return tz // 2, (yy * 4 + tz // 2, gy, lax.rem(tz, 2) * 2 + core)

    def row(n):
        tx, tc = lax.rem(xx + n // 2, 4), lax.rem(core + lax.rem(n, 2), 2)
        return (gx, tx, zlo * 2 + tc)

    loads = [
        pltpu.make_async_copy(a, b, load_sem.at[i])
        for i, (a, b) in enumerate(((cot, cot_v), (fine, fine_v), (w_down, wd_v), (w_conv, wc_v)))
    ]
    for c in loads:
        c.start()

    barrier = pltpu.get_barrier_semaphore()

    def greet(device):
        pl.semaphore_signal(barrier, inc=1, device_id=device, device_id_type=MESH)

    for s in NEIGHBOURS:
        greet(near(s))
    greet(other)

    @pl.loop(1, 16)
    def _(n):
        greet(plane(n)[2])

    @pl.loop(1, 8)
    def _(n):
        greet(column(n)[1])

    @pl.loop(1, 8)
    def _(n):
        greet(row(n))

    o0 = occupied[0, 0, 0].astype(F32)
    o1 = occupied[0, 1, 0].astype(F32)
    rows = lax.broadcasted_iota(jnp.int32, (16, 8, 128), 0)
    occ = jnp.where(rows < 8, o0, o1)
    loads[0].wait()

    @pl.loop(0, 8)
    def _(x):
        m = cot_v[x].astype(F32) * occ
        mp[x + 1, 1:17] = m.astype(BF)
        mz[0, x] = m[:, 0:1, :]
        mz[1, x] = m[:, 7:8, :]

    pl.semaphore_wait(barrier, 26 + 1 + 15 + 7 + 7)

    def halo(pad, zs, zr, ss, rs):
        copies = []
        for i, (sx, sy, sz) in enumerate(NEIGHBOURS):
            sxs = {-1: slice(1, 2), 0: slice(1, 9), 1: slice(8, 9)}[sx]
            dxs = {-1: slice(9, 10), 0: slice(1, 9), 1: slice(0, 1)}[sx]
            sys_ = {-1: slice(1, 2), 0: slice(1, 17), 1: slice(16, 17)}[sy]
            dys = {-1: slice(17, 18), 0: slice(1, 17), 1: slice(0, 1)}[sy]
            if sz == 0:
                src = pad.at[sxs, sys_]
                dst = pad.at[dxs, dys]
            else:
                src = zs.at[(sz + 1) // 2, slice(sxs.start - 1, sxs.stop - 1),
                            slice(sys_.start - 1, sys_.stop - 1)]
                dst = zr.at[(1 - sz) // 2, dxs, dys]
            copies.append(
                pltpu.make_async_remote_copy(
                    src_ref=src, dst_ref=dst, send_sem=ss.at[i], recv_sem=rs.at[i],
                    device_id=near((sx, sy, sz)), device_id_type=MESH,
                )
            )
        for c in copies:
            c.start()
        return copies

    m_copies = halo(mp, mz, mzr, mh_s, mh_r)

    loads[1].wait()
    loads[2].wait()
    patches = [
        fine_v[:, a, :, b].reshape(1024, 128) for a in range(2) for b in range(2)
    ]
    z = dot(jnp.concatenate(patches, axis=1), wd_v[...].reshape(512, 128), 1, 0)
    zval = (z.reshape(8, 16, 8, 128) * occ[None]).astype(BF)
    act = jnp.maximum(zval.astype(F32), 0.0)
    zv[...] = zval
    ap[1:9, 1:17] = act.astype(BF)
    az[0] = act[:, :, 0:1, :]
    az[1] = act[:, :, 7:8, :]
    a_copies = halo(ap, az, azr, ah_s, ah_r)
    act_t[...] = act.reshape(1024, 128).T.astype(BF)
    for i in range(4):
        patch_t[i * 128 : (i + 1) * 128] = patches[i].T

    kk = lax.broadcasted_iota(jnp.int32, (18, 8, 128), 1)
    yi = lax.broadcasted_iota(jnp.int32, (18, 8, 128), 0)
    inside_y = jnp.logical_and(
        jnp.logical_or(yi > 0, gy > 0), jnp.logical_or(yi < 17, gy < NGY - 1)
    )

    def build(pad, zr, even, odd):
        @pl.loop(0, 10)
        def _(x):
            inside_x = jnp.logical_and(
                jnp.logical_or(x > 0, gx > 0), jnp.logical_or(x < 9, gx < NGX - 1)
            )
            keep = jnp.where(jnp.logical_and(inside_y, inside_x), 1.0, 0.0)
            low = jnp.where(gz > 0, 1.0, 0.0)
            high = jnp.where(gz < NGZ - 1, 1.0, 0.0)
            m = pad[x].astype(F32)
            lo = jnp.where(kk == 0, zr[0, x] * low, pltpu.roll(m, 1, 1)) * keep
            hi = jnp.where(kk == 7, zr[1, x] * high, pltpu.roll(m, 7, 1)) * keep
            for b, v in enumerate((lo, m * keep, hi)):
                even[x, :, b * 128 : (b + 1) * 128] = v.reshape(144, 128).astype(BF)
                odd[x, :, b * 128 : (b + 1) * 128] = v[1:17].reshape(128, 128).astype(BF)

    def cut(even, odd, ox, oy):
        if oy == 1:
            return odd[ox : ox + 8].reshape(1024, 384)
        return even[ox : ox + 8, oy * 8 : oy * 8 + 128].reshape(1024, 384)

    def behind(g):
        return cut(me_v, mo_v, 2 - g // 3, 2 - g % 3)

    for c in m_copies:
        c.wait_recv()
    build(mp, mzr, me_v, mo_v)

    def conv_grads(lo, hi):
        for i in range(lo, hi):
            d = dot(act_t[...], behind(GROUPS[i]), 1, 0)
            for b in range(3):
                grads[3 * i + b] = d[:, b * 128 : (b + 1) * 128].astype(BF)

    def s0(j):
        return pltpu.make_async_remote_copy(
            src_ref=grads.at[pl.ds(8 * j + 4 - 4 * core, 4)], dst_ref=r0.at[j],
            send_sem=s0_s.at[j], recv_sem=s0_r.at[j], device_id=other, device_id_type=MESH,
        )

    def s1(j, n):
        tx, ty, device = plane(n)
        return pltpu.make_async_remote_copy(
            src_ref=p1.at[j, tx, pl.ds(pl.multiple_of(ty * 32, 32), 32)], dst_ref=r1.at[j, n],
            send_sem=s1_s.at[j, n], recv_sem=s1_r.at[j, n],
            device_id=device, device_id_type=MESH,
        )

    def s0_finish(j):
        s0(j).wait_recv()
        p1[j] = (grads[pl.ds(8 * j + 4 * core, 4)].astype(F32) + r0[j].astype(F32)).astype(BF)

        @pl.loop(1, 16)
        def _(n):
            s1(j, n).start()

    def s1_finish(j):
        @pl.loop(1, 16)
        def _(n):
            s1(j, n).wait_recv()

        total = p1[j, xx, pl.ds(pl.multiple_of(yy * 32, 32), 32)].astype(F32)
        for n in range(1, 16):
            total = total + r1[j, n].astype(F32)
        s1acc[j] = total

    conv_grads(0, 3)
    s0(0).start()
    conv_grads(3, 6)
    s0(1).start()
    s0_finish(0)

    for g in range(0, 9, 2):
        pair = [g, g + 1] if g < 8 else [8]
        left = jnp.concatenate([behind(h) for h in pair], axis=1)
        right = jnp.concatenate([wc_v[3 * h + 2 - b] for h in pair for b in range(3)], axis=1)
        if g == 0:
            loads[3].wait()
            right = jnp.concatenate([wc_v[3 * h + 2 - b] for h in pair for b in range(3)], axis=1)
            acc[...] = dot(left, right, 1, 1)
        else:
            acc[...] += dot(left, right, 1, 1)
    s0_finish(1)
    d_act = acc[...].reshape(8, 16, 8, 128)
    positive = zv[...].astype(F32) > 0
    dz = occ[None] * (cot_v[...].astype(F32) + jnp.where(positive, d_act, 0.0))
    dz_v[...] = dz.reshape(1024, 128).astype(BF)
    d = dot(patch_t[...], dz_v[...], 1, 0)
    for i in range(4):
        grads[27 + i] = d[i * 128 : (i + 1) * 128].astype(BF)
    grads[31] = jnp.zeros((128, 128), BF)
    conv_grads(6, 8)
    s0(2).start()
    conv_grads(8, 9)
    s0(3).start()
    s0_finish(2)

    s0_finish(3)
    d = dot(dz_v[...], wd_v[...].reshape(512, 128), 1, 1)
    for a in range(2):
        for b in range(2):
            i = 2 * a + b
            d_fine[:, a, :, b] = d[:, i * 128 : (i + 1) * 128].reshape(8, 16, 8, 128).astype(BF)

    for c in a_copies:
        c.wait_recv()
    build(ap, azr, ae_v, ao_v)
    for g in range(0, 9, 2):
        pair = [g, g + 1] if g < 8 else [8]
        left = jnp.concatenate([cut(ae_v, ao_v, h // 3, h % 3) for h in pair], axis=1)
        right = wc_v[3 * g : 3 * g + 3 * len(pair)].reshape(384 * len(pair), 128)
        if g == 0:
            acc[...] = dot(left, right, 1, 0)
        else:
            acc[...] += dot(left, right, 1, 0)
    out[...] = (
        zv[...].astype(F32) + occ[None] * acc[...].reshape(8, 16, 8, 128)
    ).astype(BF)

    for j in range(4):
        s1_finish(j)
    for h in range(4):
        p2[h] = jnp.concatenate([s1acc[j, h * 8 : h * 8 + 8] for j in range(4)], axis=0).astype(BF)

    def s3(n):
        h, device = column(n)
        return pltpu.make_async_remote_copy(
            src_ref=p2.at[h], dst_ref=r3.at[n], send_sem=s3_s.at[n], recv_sem=s3_r.at[n],
            device_id=device, device_id_type=MESH,
        )

    @pl.loop(1, 8)
    def _(n):
        s3(n).start()

    @pl.loop(1, 8)
    def _(n):
        s3(n).wait_recv()

    total = p2[zhi].astype(F32)
    for n in range(1, 8):
        total = total + r3[n].astype(F32)
    mine = total.astype(BF)
    p3[...] = mine
    r4[xx * 2 + core] = mine

    def s4(n):
        return pltpu.make_async_remote_copy(
            src_ref=p3, dst_ref=r4.at[xx * 2 + core], send_sem=s4_s.at[n], recv_sem=s4_r.at[n],
            device_id=row(n), device_id_type=MESH,
        )

    @pl.loop(1, 8)
    def _(n):
        s4(n).start()

    @pl.loop(1, 8)
    def _(n):
        s4(n).wait_recv()

    scale = float(262144) ** -0.5
    for x in range(4):
        for c in range(2):
            v = r4[x * 2 + c].astype(F32) * scale
            for j in range(4):
                slot = 8 * j + 4 * c + x
                if slot == 31:
                    continue
                tap = SLOTS[slot]
                if tap < 27:
                    d_wconv[tap] = v[8 * j : 8 * j + 8]
                else:
                    d_wdown[tap - 27] = v[8 * j : 8 * j + 8]

    for c in m_copies + a_copies:
        c.wait_send()
    for j in range(4):
        s0(j).wait_send()

        @pl.loop(1, 16)
        def _(n):
            s1(j, n).wait_send()

    @pl.loop(1, 8)
    def _(n):
        s3(n).wait_send()
        s4(n).wait_send()


def body(fine, occupied, w_down, w_conv, cotangent):
    fine = fine.reshape(8, 2, 16, 2, 8, 128)
    vm = pltpu.VMEM
    dma = pltpu.SemaphoreType.DMA
    scratch = [
        vm(fine.shape, BF), vm(w_down.shape, BF), vm(w_conv.shape, BF), vm(cotangent.shape, BF),
        vm((10, 18, 8, 128), BF), vm((10, 18, 8, 128), BF),
        vm((2, 8, 16, 1, 128), F32), vm((2, 8, 16, 1, 128), F32),
        vm((2, 10, 18, 1, 128), F32), vm((2, 10, 18, 1, 128), F32),
        vm((10, 144, 384), BF), vm((10, 128, 384), BF),
        vm((10, 144, 384), BF), vm((10, 128, 384), BF),
        vm((8, 16, 8, 128), BF),
        vm((128, 1024), BF), vm((512, 1024), BF),
        vm((1024, 128), F32), vm((1024, 128), BF),
        vm((32, 128, 128), BF),
        vm((4, 4, 128, 128), BF), vm((4, 4, 128, 128), BF),
        vm((4, 16, 32, 128), BF), vm((4, 32, 128), F32),
        vm((4, 32, 128), BF), vm((8, 32, 128), BF),
        vm((32, 128), BF), vm((8, 32, 128), BF),
        dma((4,)), dma((26,)), dma((26,)), dma((26,)), dma((26,)),
        dma((4,)), dma((4,)), dma((4, 16)), dma((4, 16)),
        dma((8,)), dma((8,)), dma((8,)), dma((8,)),
    ]
    anym = pl.BlockSpec(memory_space=pl.ANY)
    vmem = pl.BlockSpec(memory_space=pltpu.VMEM)
    smem = pl.BlockSpec(memory_space=pltpu.SMEM)
    out, d_fine, d_wconv, d_wdown = pl.pallas_call(
        kernel,
        out_shape=(
            jax.ShapeDtypeStruct(cotangent.shape, BF),
            jax.ShapeDtypeStruct(fine.shape, BF),
            jax.ShapeDtypeStruct((27, 8, 128), F32),
            jax.ShapeDtypeStruct((4, 8, 128), F32),
        ),
        in_specs=[anym, smem, anym, anym, anym],
        out_specs=(vmem, vmem, vmem, vmem),
        scratch_shapes=scratch,
        compiler_params=pltpu.CompilerParams(
            collective_id=0, has_side_effects=True, vmem_limit_bytes=48 * 1024 * 1024
        ),
    )(fine, occupied, w_down, w_conv, cotangent)
    return out, d_fine.reshape(16, 32, 8, 128), d_wconv, d_wdown


def solution(mesh):
    in_specs = (P("gx", "gy", "gz", None), P("gx", "gy", "gz"), P(), P(), P("gx", "gy", "gz", None))
    out_specs = (
        P("gx", "gy", "gz", None),
        P("gx", "gy", "gz", None),
        P(None, "gx", None),
        P(None, "gx", None),
    )
    return jax.shard_map(body, mesh=mesh, in_specs=in_specs, out_specs=out_specs, check_vma=False)
```

```python
import jax
import jax.numpy as jnp
from jax import lax
from jax.experimental import pallas as pl
from jax.experimental.pallas import tpu as pltpu
from jax.sharding import PartitionSpec as P

BF = jnp.bfloat16
F32 = jnp.float32
MESH = pl.DeviceIdType.MESH

NGX, NGY, NGZ = 16, 4, 4
NEIGHBOURS = [
    (sx, sy, sz)
    for sx in (-1, 1, 0)
    for sz in (-1, 1, 0)
    for sy in (-1, 1, 0)
    if (sx, sy, sz) != (0, 0, 0)
]
FAR = 18
GROUPS = [3, 4, 5, 0, 1, 2, 6, 7, 8]
SLOTS = [3 * g + 2 - b for g in GROUPS for b in range(3)] + [27, 28, 29, 30]


def dot(a, b, ca, cb):
    return lax.dot_general(a, b, (((ca,), (cb,)), ((), ())), preferred_element_type=F32)


def kernel(
    fine, occupied, w_down, w_conv, cot,
    out_h, d_fine_h, d_wconv_h, d_wdown_h,
    out, d_fine, d_wconv, d_wdown, store_sem, fine_v, wd_v, wc_v, cot_v,
    mp, ap, mz, az, mzr, azr, me_v, mo_v, ae_v, ao_v,
    zv, act_t, patch_t, acc, dz_v, grads,
    r0, p1, r1, p2, r3, p3, r4, gsum, dsum,
    occ_v, load_sem, halo_s, mh_r, ah_r, s0_s, s0_r, s1_s, s1_r, s3_s, s3_r, s4_s, s4_r,
):
    gx, gy, gz = lax.axis_index("gx"), lax.axis_index("gy"), lax.axis_index("gz")
    yy, zhi, xx = gx // 4, lax.rem(gx, 4), gy
    zlo, core = gz // 2, lax.rem(gz, 2)
    zz = zhi * 2 + zlo

    def near(s):
        return (
            lax.rem(gx + s[0] + NGX, NGX),
            lax.rem(gy + s[1] + NGY, NGY),
            lax.rem(gz + s[2] + NGZ, NGZ),
        )

    other = (gx, gy, gz + 1 - 2 * core)

    def plane(n):
        tx, ty = lax.rem(xx + lax.rem(n, 4), 4), lax.rem(yy + n // 4, 4)
        return tx, ty, (ty * 4 + zhi, tx, gz)

    def column(n):
        tz = lax.rem(zz + n, 8)
        return tz // 2, (yy * 4 + tz // 2, gy, lax.rem(tz, 2) * 2 + core)

    def row(n):
        tx, tc = lax.rem(xx + n // 2, 4), lax.rem(core + lax.rem(n, 2), 2)
        return (gx, tx, zlo * 2 + tc)

    loads = [
        pltpu.make_async_copy(a, b, load_sem.at[i])
        for i, (a, b) in enumerate(((cot, cot_v), (fine, fine_v), (w_down, wd_v), (w_conv, wc_v), (occupied, occ_v)))
    ]
    for c in loads:
        c.start()

    barrier = pltpu.get_barrier_semaphore()

    def greet(device):
        pl.semaphore_signal(barrier, inc=1, device_id=device, device_id_type=MESH)

    for s in NEIGHBOURS:
        greet(near(s))
    greet(other)

    @pl.loop(1, 16)
    def _(n):
        greet(plane(n)[2])

    @pl.loop(1, 8)
    def _(n):
        greet(column(n)[1])

    @pl.loop(1, 8)
    def _(n):
        greet(row(n))

    loads[4].wait()
    o0 = occ_v[0, 0, 0].astype(F32)
    o1 = occ_v[0, 0, 1].astype(F32)
    rows = lax.broadcasted_iota(jnp.int32, (16, 8, 128), 0)
    occ = jnp.where(rows < 8, o0, o1)
    loads[0].wait()

    @pl.loop(0, 8)
    def _(x):
        m = cot_v[x].astype(F32) * occ
        mp[x + 1, 1:17] = m.astype(BF)
        mz[0, x] = m[:, 0:1, :]
        mz[1, x] = m[:, 7:8, :]

    pl.semaphore_wait(barrier, 26 + 1 + 15 + 7 + 7)

    def halo(pad, zs, zr, rs):
        copies = []
        for i, (sx, sy, sz) in enumerate(NEIGHBOURS):
            sxs = {-1: slice(1, 2), 0: slice(1, 9), 1: slice(8, 9)}[sx]
            dxs = {-1: slice(9, 10), 0: slice(1, 9), 1: slice(0, 1)}[sx]
            sys_ = {-1: slice(1, 2), 0: slice(1, 17), 1: slice(16, 17)}[sy]
            dys = {-1: slice(17, 18), 0: slice(1, 17), 1: slice(0, 1)}[sy]
            if sz == 0:
                src = pad.at[sxs, sys_]
                dst = pad.at[dxs, dys]
            else:
                src = zs.at[(sz + 1) // 2, slice(sxs.start - 1, sxs.stop - 1),
                            slice(sys_.start - 1, sys_.stop - 1)]
                dst = zr.at[(1 - sz) // 2, dxs, dys]
            copies.append(
                pltpu.make_async_remote_copy(
                    src_ref=src, dst_ref=dst, send_sem=halo_s, recv_sem=rs.at[0 if i < FAR else 1],
                    device_id=near((sx, sy, sz)), device_id_type=MESH,
                )
            )
        for c in copies:
            c.start()

    def landed(sem, ref):
        pltpu.make_async_copy(ref, ref, sem).wait()

    far_bytes, near_bytes = acc.at[0:216], acc.at[0:352]

    halo(mp, mz, mzr, mh_r)

    loads[1].wait()
    loads[2].wait()
    patches = [
        fine_v[:, a, :, b].reshape(1024, 128) for a in range(2) for b in range(2)
    ]
    z = dot(jnp.concatenate(patches, axis=1), wd_v[...].reshape(512, 128), 1, 0)
    zval = (z.reshape(8, 16, 8, 128) * occ[None]).astype(BF)
    act = jnp.maximum(zval.astype(F32), 0.0)
    zv[...] = zval
    ap[1:9, 1:17] = act.astype(BF)
    az[0] = act[:, :, 0:1, :]
    az[1] = act[:, :, 7:8, :]
    halo(ap, az, azr, ah_r)
    act_t[...] = act.reshape(1024, 128).T.astype(BF)
    for i in range(4):
        patch_t[i * 128 : (i + 1) * 128] = patches[i].T

    kk = lax.broadcasted_iota(jnp.int32, (18, 8, 128), 1)
    yi = lax.broadcasted_iota(jnp.int32, (18, 8, 128), 0)
    inside_y = jnp.logical_and(
        jnp.logical_or(yi > 0, gy > 0), jnp.logical_or(yi < 17, gy < NGY - 1)
    )

    def build(pad, zr, even, odd, first, last):
        @pl.loop(first, last)
        def _(x):
            inside_x = jnp.logical_and(
                jnp.logical_or(x > 0, gx > 0), jnp.logical_or(x < 9, gx < NGX - 1)
            )
            keep = jnp.where(jnp.logical_and(inside_y, inside_x), 1.0, 0.0)
            low = jnp.where(gz > 0, 1.0, 0.0)
            high = jnp.where(gz < NGZ - 1, 1.0, 0.0)
            m = pad[x].astype(F32)
            lo = jnp.where(kk == 0, zr[0, x] * low, pltpu.roll(m, 1, 1)) * keep
            hi = jnp.where(kk == 7, zr[1, x] * high, pltpu.roll(m, 7, 1)) * keep
            for b, v in enumerate((lo, m * keep, hi)):
                even[x, :, b * 128 : (b + 1) * 128] = v.reshape(144, 128).astype(BF)
                odd[x, :, b * 128 : (b + 1) * 128] = v[1:17].reshape(128, 128).astype(BF)

    def cut(even, odd, first, count, oy):
        if oy == 1:
            return odd[first : first + count].reshape(count * 128, 384)
        return even[first : first + count, oy * 8 : oy * 8 + 128].reshape(count * 128, 384)

    own = {0: (2, 0, 7), 1: (1, 0, 8), 2: (1, 1, 7)}
    edge = {0: (9, 7, 1), 2: (0, 0, 1)}

    def conv_grad(g, where):
        first, mine, count = where[g // 3]
        return dot(
            act_t[:, mine * 128 : (mine + count) * 128],
            cut(me_v, mo_v, first, count, 2 - g % 3), 1, 0,
        )

    def back(dx, where):
        first, mine, count = where[dx]
        left = jnp.concatenate(
            [cut(me_v, mo_v, first, count, 2 - dy) for dy in range(3)], axis=1
        )
        right = jnp.concatenate(
            [wc_v[9 * dx + 3 * dy + 2 - b] for dy in range(3) for b in range(3)], axis=1
        )
        return slice(mine * 128, (mine + count) * 128), dot(left, right, 1, 1)

    def dz_of(first, last):
        d_act = acc[first * 128 : last * 128].reshape(last - first, 16, 8, 128)
        positive = zv[first:last].astype(F32) > 0
        dz = occ[None] * (cot_v[first:last].astype(F32) + jnp.where(positive, d_act, 0.0))
        dz_v[first * 128 : last * 128] = dz.reshape((last - first) * 128, 128).astype(BF)

    def s0(j):
        return pltpu.make_async_remote_copy(
            src_ref=grads.at[pl.ds(8 * j + 4 - 4 * core, 4)], dst_ref=r0.at[j],
            send_sem=s0_s, recv_sem=s0_r.at[j], device_id=other, device_id_type=MESH,
        )

    def s1(j, n):
        tx, ty, device = plane(n)
        return pltpu.make_async_remote_copy(
            src_ref=p1.at[j, tx, pl.ds(pl.multiple_of(ty * 32, 32), 32)], dst_ref=r1.at[j, n],
            send_sem=s1_s, recv_sem=s1_r.at[j],
            device_id=device, device_id_type=MESH,
        )

    def s0_finish(j):
        s0(j).wait_recv()
        p1[j] = (grads[pl.ds(8 * j + 4 * core, 4)].astype(F32) + r0[j].astype(F32)).astype(BF)

        @pl.loop(1, 16)
        def _(n):
            s1(j, n).start()

    def s1_finish(j):
        landed(s1_r.at[j], r1.at[j, pl.ds(1, 15)])

        total = p1[j, xx, pl.ds(pl.multiple_of(yy * 32, 32), 32)].astype(F32)
        for n in range(1, 16):
            total = total + r1[j, n].astype(F32)
        return total

    def s3(i, n):
        h, device = column(n)
        return pltpu.make_async_remote_copy(
            src_ref=p2.at[i, h], dst_ref=r3.at[i, n],
            send_sem=s3_s, recv_sem=s3_r.at[i],
            device_id=device, device_id_type=MESH,
        )

    def s4(i, n):
        return pltpu.make_async_remote_copy(
            src_ref=p3.at[i], dst_ref=r4.at[i, xx * 2 + core],
            send_sem=s4_s, recv_sem=s4_r.at[i],
            device_id=row(n), device_id_type=MESH,
        )

    def s3_start(i):
        low, high = s1_finish(2 * i), s1_finish(2 * i + 1)
        for h in range(4):
            p2[i, h] = jnp.concatenate(
                [low[h * 8 : h * 8 + 8], high[h * 8 : h * 8 + 8]], axis=0
            ).astype(BF)

        @pl.loop(1, 8)
        def _(n):
            s3(i, n).start()

    def s4_start(i):
        landed(s3_r.at[i], r3.at[i, pl.ds(1, 7)])

        total = p2[i, zhi].astype(F32)
        for n in range(1, 8):
            total = total + r3[i, n].astype(F32)
        mine = total.astype(BF)
        p3[i] = mine
        r4[i, xx * 2 + core] = mine

        @pl.loop(1, 8)
        def _(n):
            s4(i, n).start()

    def s4_finish(i):
        landed(s4_r.at[i], r4.at[i, pl.ds(1, 7)])

        for x in range(4):
            for c in range(2):
                v = r4[i, x * 2 + c].astype(F32) * (262144.0 ** -0.5)
                for h in range(2):
                    slot = 8 * (2 * i + h) + 4 * c + x
                    if slot == 31:
                        continue
                    tap = SLOTS[slot]
                    if tap < 27:
                        d_wconv[tap] = v[8 * h : 8 * h + 8]
                    else:
                        d_wdown[tap - 27] = v[8 * h : 8 * h + 8]

    def put(i, d):
        for b in range(3):
            grads[3 * i + b] = d[:, b * 128 : (b + 1) * 128].astype(BF)

    landed(mh_r.at[1], near_bytes)
    build(mp, mzr, me_v, mo_v, 1, 9)
    for i in range(3):
        put(i, conv_grad(GROUPS[i], own))
    s0(0).start()
    loads[3].wait()
    acc[...] = back(1, own)[1]
    s0_finish(0)
    for i in range(3, 9):
        gsum[i - 3] = conv_grad(GROUPS[i], own)
    for dx in (0, 2):
        where, d = back(dx, own)
        acc[where] += d
    dz_of(1, 7)
    dsum[...] = dot(patch_t[:, 128:896], dz_v[128:896], 1, 0)

    landed(mh_r.at[0], far_bytes)
    build(mp, mzr, me_v, mo_v, 0, 1)
    build(mp, mzr, me_v, mo_v, 9, 10)
    for i in range(3, 9):
        put(i, gsum[i - 3] + conv_grad(GROUPS[i], edge))
        if i == 5:
            s0(1).start()
        if i == 7:
            s0(2).start()
    for dx in (0, 2):
        where, d = back(dx, edge)
        acc[where] += d
    dz_of(0, 1)
    dz_of(7, 8)
    d = dsum[...] + dot(
        jnp.concatenate([patch_t[:, :128], patch_t[:, 896:]], axis=1),
        jnp.concatenate([dz_v[:128], dz_v[896:]], axis=0), 1, 0,
    )
    for i in range(4):
        grads[27 + i] = d[i * 128 : (i + 1) * 128].astype(BF)
    grads[31] = jnp.zeros((128, 128), BF)
    s0(3).start()
    s0_finish(1)
    s0_finish(2)
    s0_finish(3)

    d = dot(dz_v[...], wd_v[...].reshape(512, 128), 1, 1)
    for a in range(2):
        for b in range(2):
            i = 2 * a + b
            d_fine[:, a, :, b] = d[:, i * 128 : (i + 1) * 128].reshape(8, 16, 8, 128).astype(BF)

    def store(i):
        pairs = ((out, out_h), (d_fine, d_fine_h), (d_wconv, d_wconv_h), (d_wdown, d_wdown_h))
        return pltpu.make_async_copy(*pairs[i], store_sem.at[i])

    store(1).start()

    landed(ah_r.at[0], far_bytes)
    landed(ah_r.at[1], near_bytes)
    build(ap, azr, ae_v, ao_v, 0, 10)
    s3_start(0)
    for g in range(0, 9, 2):
        pair = [g, g + 1] if g < 8 else [8]
        left = jnp.concatenate([cut(ae_v, ao_v, h // 3, 8, h % 3) for h in pair], axis=1)
        right = wc_v[3 * g : 3 * g + 3 * len(pair)].reshape(384 * len(pair), 128)
        if g == 0:
            acc[...] = dot(left, right, 1, 0)
        else:
            acc[...] += dot(left, right, 1, 0)
    out[...] = (
        zv[...].astype(F32) + occ[None] * acc[...].reshape(8, 16, 8, 128)
    ).astype(BF)
    store(0).start()
    s3_start(1)
    s4_start(0)
    s4_start(1)
    s4_finish(0)
    s4_finish(1)
    store(2).start()
    store(3).start()

    landed(halo_s, acc.at[0:568])
    landed(halo_s, acc.at[0:568])
    landed(s0_s, r0)
    landed(s1_s, r1.at[:, pl.ds(1, 15)])
    landed(s3_s, r3.at[:, pl.ds(1, 7)])
    landed(s4_s, r4.at[:, pl.ds(1, 7)])
    for i in range(4):
        store(i).wait()


PARTS = (1, 4, 1, 1)


def publish_kernel(*refs):
    ins, outs, held = refs[:4], refs[4:8], refs[8:12]
    load_sem, store_sem = refs[12:]
    pieces = []
    for i, parts in enumerate(PARTS):
        size = ins[i].shape[0] // parts
        for p in range(parts):
            at = pl.ds(p * size, size)
            k = len(pieces)
            pieces.append((
                pltpu.make_async_copy(ins[i].at[at], held[i].at[at], load_sem.at[k]),
                pltpu.make_async_copy(held[i].at[at], outs[i].at[at], store_sem.at[k]),
            ))
    for load, _ in pieces:
        load.start()
    for load, store in pieces:
        load.wait()
        store.start()
    for _, store in pieces:
        store.wait()


def publish(*arrays):
    anym = pl.BlockSpec(memory_space=pl.ANY)
    return pl.pallas_call(
        publish_kernel,
        out_shape=tuple(jax.ShapeDtypeStruct(a.shape, a.dtype) for a in arrays),
        in_specs=[anym] * 4,
        out_specs=(anym,) * 4,
        scratch_shapes=[pltpu.VMEM(a.shape, a.dtype) for a in arrays]
        + [pltpu.SemaphoreType.DMA((sum(PARTS),))] * 2,
        compiler_params=pltpu.CompilerParams(vmem_limit_bytes=56 * 1024 * 1024),
    )(*arrays)


def body(fine, occupied, w_down, w_conv, cotangent):
    fine = fine.reshape(8, 2, 16, 2, 8, 128)
    vm = pltpu.VMEM
    dma = pltpu.SemaphoreType.DMA
    scratch = [
        vm(cotangent.shape, BF), vm(fine.shape, BF), vm((27, 8, 128), F32), vm((4, 8, 128), F32),
        dma((4,)),
        vm(fine.shape, BF), vm(w_down.shape, BF), vm(w_conv.shape, BF), vm(cotangent.shape, BF),
        vm((10, 18, 8, 128), BF), vm((10, 18, 8, 128), BF),
        vm((2, 8, 16, 1, 128), F32), vm((2, 8, 16, 1, 128), F32),
        vm((2, 10, 18, 1, 128), F32), vm((2, 10, 18, 1, 128), F32),
        vm((10, 144, 384), BF), vm((10, 128, 384), BF),
        vm((10, 144, 384), BF), vm((10, 128, 384), BF),
        vm((8, 16, 8, 128), BF),
        vm((128, 1024), BF), vm((512, 1024), BF),
        vm((1024, 128), F32), vm((1024, 128), BF),
        vm((32, 128, 128), BF),
        vm((4, 4, 128, 128), BF), vm((4, 4, 128, 128), BF),
        vm((4, 16, 32, 128), BF),
        vm((2, 4, 16, 128), BF), vm((2, 8, 16, 128), BF),
        vm((2, 16, 128), BF), vm((2, 8, 16, 128), BF),
        vm((6, 128, 384), F32), vm((512, 128), F32),
        pltpu.SMEM((1, 1, 2), jnp.int32),
        dma((5,)), dma, dma((2,)), dma((2,)),
        dma, dma((4,)), dma, dma((4,)), dma, dma((2,)), dma, dma((2,)),
    ]
    anym = pl.BlockSpec(memory_space=pl.ANY)
    out, d_fine, d_wconv, d_wdown = pl.pallas_call(
        kernel,
        out_shape=(
            jax.ShapeDtypeStruct(cotangent.shape, BF),
            jax.ShapeDtypeStruct(fine.shape, BF),
            jax.ShapeDtypeStruct((27, 8, 128), F32),
            jax.ShapeDtypeStruct((4, 8, 128), F32),
        ),
        in_specs=[anym, anym, anym, anym, anym],
        out_specs=(anym, anym, anym, anym),
        scratch_shapes=scratch,
        compiler_params=pltpu.CompilerParams(
            collective_id=0, has_side_effects=True, vmem_limit_bytes=56 * 1024 * 1024
        ),
    )(fine, jnp.transpose(occupied, (0, 2, 1)), w_down, w_conv, cotangent)
    out, d_fine, d_wconv, d_wdown = publish(out, d_fine, d_wconv, d_wdown)
    return out, d_fine.reshape(16, 32, 8, 128), d_wconv, d_wdown


def solution(mesh):
    in_specs = (P("gx", "gy", "gz", None), P("gx", "gy", "gz"), P(), P(), P("gx", "gy", "gz", None))
    out_specs = (
        P("gx", "gy", "gz", None),
        P("gx", "gy", "gz", None),
        P(None, "gx", None),
        P(None, "gx", None),
    )
    return jax.shard_map(body, mesh=mesh, in_specs=in_specs, out_specs=out_specs, check_vma=False)
```

```python
import jax
import jax.numpy as jnp
from jax import lax
from jax.experimental import pallas as pl
from jax.experimental.pallas import tpu as pltpu
from jax.sharding import PartitionSpec as P

BF = jnp.bfloat16
F32 = jnp.float32
MESH = pl.DeviceIdType.MESH

NGX, NGY, NGZ = 16, 4, 4
NEIGHBOURS = [
    (sx, sy, sz)
    for sx in (0, -1, 1)
    for sz in (-1, 1, 0)
    for sy in (-1, 1, 0)
    if (sx, sy, sz) != (0, 0, 0)
]
NEAR = 8
GROUPS = [3, 4, 5, 0, 1, 2, 6, 7, 8]
SLOTS = [3 * g + 2 - b for g in GROUPS for b in range(3)] + [27, 28, 29, 30]


def dot(a, b, ca, cb):
    return lax.dot_general(a, b, (((ca,), (cb,)), ((), ())), preferred_element_type=F32)


def kernel(
    fine, occupied, w_down, w_conv, cot,
    out, d_fine, d_wconv, d_wdown,
    fine_v, wd_v, wc_v, cot_v,
    mp, ap, mz, az, mzr, azr, me_v, mo_v, ae_v, ao_v,
    zv, act_t, patch_t, acc, dz_v, grads,
    r0, p1, r1, p2, r3, p3, r4, gsum, dsum,
    occ_v, load_sem, halo_s, mh_r, ah_r, s0_s, s0_r, s1_s, s1_r, s3_s, s3_r, s4_s, s4_r,
):
    gx, gy, gz = lax.axis_index("gx"), lax.axis_index("gy"), lax.axis_index("gz")
    yy, zhi, xx = gx // 4, lax.rem(gx, 4), gy
    zlo, core = gz // 2, lax.rem(gz, 2)
    zz = zhi * 2 + zlo

    def near(s):
        return (
            lax.rem(gx + s[0] + NGX, NGX),
            lax.rem(gy + s[1] + NGY, NGY),
            lax.rem(gz + s[2] + NGZ, NGZ),
        )

    other = (gx, gy, gz + 1 - 2 * core)

    def plane(n):
        tx, ty = lax.rem(xx + lax.rem(n, 4), 4), lax.rem(yy + n // 4, 4)
        return tx, ty, (ty * 4 + zhi, tx, gz)

    def column(n):
        tz = lax.rem(zz + n, 8)
        return tz // 2, (yy * 4 + tz // 2, gy, lax.rem(tz, 2) * 2 + core)

    def row(n):
        tx, tc = lax.rem(xx + n // 2, 4), lax.rem(core + lax.rem(n, 2), 2)
        return (gx, tx, zlo * 2 + tc)

    loads = [
        pltpu.make_async_copy(a, b, load_sem.at[i])
        for i, (a, b) in enumerate(((cot, cot_v), (fine, fine_v), (w_down, wd_v), (w_conv, wc_v), (occupied, occ_v)))
    ]
    for c in loads:
        c.start()

    barrier = pltpu.get_barrier_semaphore()

    def greet(device):
        pl.semaphore_signal(barrier, inc=1, device_id=device, device_id_type=MESH)

    for s in NEIGHBOURS:
        greet(near(s))
    greet(other)

    @pl.loop(1, 16)
    def _(n):
        greet(plane(n)[2])

    @pl.loop(1, 8)
    def _(n):
        greet(column(n)[1])

    @pl.loop(1, 8)
    def _(n):
        greet(row(n))

    loads[4].wait()
    o0 = occ_v[0, 0, 0].astype(F32)
    o1 = occ_v[0, 0, 1].astype(F32)
    rows = lax.broadcasted_iota(jnp.int32, (16, 8, 128), 0)
    occ = jnp.where(rows < 8, o0, o1)
    loads[0].wait()

    @pl.loop(0, 8)
    def _(x):
        m = cot_v[x].astype(F32) * occ
        mp[x + 1, 1:17] = m.astype(BF)
        mz[0, x] = m[:, 0:1, :]
        mz[1, x] = m[:, 7:8, :]

    pl.semaphore_wait(barrier, 26 + 1 + 15 + 7 + 7)

    def halo(pad, zs, zr, rs):
        copies = []
        for i, (sx, sy, sz) in enumerate(NEIGHBOURS):
            sxs = {-1: slice(1, 2), 0: slice(1, 9), 1: slice(8, 9)}[sx]
            dxs = {-1: slice(9, 10), 0: slice(1, 9), 1: slice(0, 1)}[sx]
            sys_ = {-1: slice(1, 2), 0: slice(1, 17), 1: slice(16, 17)}[sy]
            dys = {-1: slice(17, 18), 0: slice(1, 17), 1: slice(0, 1)}[sy]
            if sz == 0:
                src = pad.at[sxs, sys_]
                dst = pad.at[dxs, dys]
            else:
                src = zs.at[(sz + 1) // 2, slice(sxs.start - 1, sxs.stop - 1),
                            slice(sys_.start - 1, sys_.stop - 1)]
                dst = zr.at[(1 - sz) // 2, dxs, dys]
            copies.append(
                pltpu.make_async_remote_copy(
                    src_ref=src, dst_ref=dst, send_sem=halo_s, recv_sem=rs.at[1 if i < NEAR else 0],
                    device_id=near((sx, sy, sz)), device_id_type=MESH,
                )
            )
        for c in copies:
            c.start()

    def landed(sem, ref):
        pltpu.make_async_copy(ref, ref, sem).wait()

    far_bytes, near_bytes = acc.at[0:216], acc.at[0:352]

    halo(mp, mz, mzr, mh_r)

    loads[1].wait()
    loads[2].wait()
    patches = [
        fine_v[:, a, :, b].reshape(1024, 128) for a in range(2) for b in range(2)
    ]
    z = dot(jnp.concatenate(patches, axis=1), wd_v[...].reshape(512, 128), 1, 0)
    zval = (z.reshape(8, 16, 8, 128) * occ[None]).astype(BF)
    act = jnp.maximum(zval.astype(F32), 0.0)
    zv[...] = zval
    ap[1:9, 1:17] = act.astype(BF)
    az[0] = act[:, :, 0:1, :]
    az[1] = act[:, :, 7:8, :]
    act_t[...] = act.reshape(1024, 128).T.astype(BF)
    for i in range(4):
        patch_t[i * 128 : (i + 1) * 128] = patches[i].T

    kk = lax.broadcasted_iota(jnp.int32, (18, 8, 128), 1)
    yi = lax.broadcasted_iota(jnp.int32, (18, 8, 128), 0)
    inside_y = jnp.logical_and(
        jnp.logical_or(yi > 0, gy > 0), jnp.logical_or(yi < 17, gy < NGY - 1)
    )

    def build(pad, zr, even, odd, first, last):
        @pl.loop(first, last)
        def _(x):
            inside_x = jnp.logical_and(
                jnp.logical_or(x > 0, gx > 0), jnp.logical_or(x < 9, gx < NGX - 1)
            )
            keep = jnp.where(jnp.logical_and(inside_y, inside_x), 1.0, 0.0)
            low = jnp.where(gz > 0, 1.0, 0.0)
            high = jnp.where(gz < NGZ - 1, 1.0, 0.0)
            m = pad[x].astype(F32)
            lo = jnp.where(kk == 0, zr[0, x] * low, pltpu.roll(m, 1, 1)) * keep
            hi = jnp.where(kk == 7, zr[1, x] * high, pltpu.roll(m, 7, 1)) * keep
            for b, v in enumerate((lo, m * keep, hi)):
                even[x, :, b * 128 : (b + 1) * 128] = v.reshape(144, 128).astype(BF)
                odd[x, :, b * 128 : (b + 1) * 128] = v[1:17].reshape(128, 128).astype(BF)

    def cut(even, odd, first, count, oy):
        if oy == 1:
            return odd[first : first + count].reshape(count * 128, 384)
        return even[first : first + count, oy * 8 : oy * 8 + 128].reshape(count * 128, 384)

    own = {0: (2, 0, 7), 1: (1, 0, 8), 2: (1, 1, 7)}
    edge = {0: (9, 7, 1), 2: (0, 0, 1)}

    def conv_grad(g, where):
        first, mine, count = where[g // 3]
        return dot(
            act_t[:, mine * 128 : (mine + count) * 128],
            cut(me_v, mo_v, first, count, 2 - g % 3), 1, 0,
        )

    def back(dx, where):
        first, mine, count = where[dx]
        left = jnp.concatenate(
            [cut(me_v, mo_v, first, count, 2 - dy) for dy in range(3)], axis=1
        )
        right = jnp.concatenate(
            [wc_v[9 * dx + 3 * dy + 2 - b] for dy in range(3) for b in range(3)], axis=1
        )
        return slice(mine * 128, (mine + count) * 128), dot(left, right, 1, 1)

    def dz_of(first, last):
        d_act = acc[first * 128 : last * 128].reshape(last - first, 16, 8, 128)
        positive = zv[first:last].astype(F32) > 0
        dz = occ[None] * (cot_v[first:last].astype(F32) + jnp.where(positive, d_act, 0.0))
        dz_v[first * 128 : last * 128] = dz.reshape((last - first) * 128, 128).astype(BF)

    def s0(j):
        return pltpu.make_async_remote_copy(
            src_ref=grads.at[pl.ds(8 * j + 4 - 4 * core, 4)], dst_ref=r0.at[j],
            send_sem=s0_s, recv_sem=s0_r.at[j], device_id=other, device_id_type=MESH,
        )

    def s1(j, n):
        tx, ty, device = plane(n)
        return pltpu.make_async_remote_copy(
            src_ref=p1.at[j, tx, pl.ds(pl.multiple_of(ty * 32, 32), 32)], dst_ref=r1.at[j, n],
            send_sem=s1_s, recv_sem=s1_r.at[j],
            device_id=device, device_id_type=MESH,
        )

    def s0_finish(j):
        s0(j).wait_recv()
        p1[j] = (grads[pl.ds(8 * j + 4 * core, 4)].astype(F32) + r0[j].astype(F32)).astype(BF)

        @pl.loop(1, 16)
        def _(n):
            s1(j, n).start()

    def s1_finish(j):
        landed(s1_r.at[j], r1.at[j, pl.ds(1, 15)])

        total = p1[j, xx, pl.ds(pl.multiple_of(yy * 32, 32), 32)].astype(F32)
        for n in range(1, 16):
            total = total + r1[j, n].astype(F32)
        return total

    def s3(i, n):
        h, device = column(n)
        return pltpu.make_async_remote_copy(
            src_ref=p2.at[i, h], dst_ref=r3.at[i, n],
            send_sem=s3_s, recv_sem=s3_r.at[i],
            device_id=device, device_id_type=MESH,
        )

    def s4(i, n):
        return pltpu.make_async_remote_copy(
            src_ref=p3.at[i], dst_ref=r4.at[i, xx * 2 + core],
            send_sem=s4_s, recv_sem=s4_r.at[i],
            device_id=row(n), device_id_type=MESH,
        )

    def s3_start(i):
        low, high = s1_finish(2 * i), s1_finish(2 * i + 1)
        for h in range(4):
            p2[i, h] = jnp.concatenate(
                [low[h * 8 : h * 8 + 8], high[h * 8 : h * 8 + 8]], axis=0
            ).astype(BF)

        @pl.loop(1, 8)
        def _(n):
            s3(i, n).start()

    def s4_start(i):
        landed(s3_r.at[i], r3.at[i, pl.ds(1, 7)])

        total = p2[i, zhi].astype(F32)
        for n in range(1, 8):
            total = total + r3[i, n].astype(F32)
        mine = total.astype(BF)
        p3[i] = mine
        r4[i, xx * 2 + core] = mine

        @pl.loop(1, 8)
        def _(n):
            s4(i, n).start()

    def s4_finish(i):
        landed(s4_r.at[i], r4.at[i, pl.ds(1, 7)])

        for x in range(4):
            for c in range(2):
                v = r4[i, x * 2 + c].astype(F32) * (262144.0 ** -0.5)
                for h in range(2):
                    slot = 8 * (2 * i + h) + 4 * c + x
                    if slot == 31:
                        continue
                    tap = SLOTS[slot]
                    if tap < 27:
                        d_wconv[tap] = v[8 * h : 8 * h + 8]
                    else:
                        d_wdown[tap - 27] = v[8 * h : 8 * h + 8]

    def put(i, d):
        for b in range(3):
            grads[3 * i + b] = d[:, b * 128 : (b + 1) * 128].astype(BF)

    landed(mh_r.at[1], near_bytes)
    build(mp, mzr, me_v, mo_v, 1, 9)
    for i in range(3):
        put(i, conv_grad(GROUPS[i], own))
    s0(0).start()
    loads[3].wait()
    acc[...] = back(1, own)[1]
    s0_finish(0)
    for i in range(3, 9):
        gsum[i - 3] = conv_grad(GROUPS[i], own)
    for dx in (0, 2):
        where, d = back(dx, own)
        acc[where] += d
    dz_of(1, 7)
    dsum[...] = dot(patch_t[:, 128:896], dz_v[128:896], 1, 0)

    landed(mh_r.at[0], far_bytes)
    halo(ap, az, azr, ah_r)
    build(mp, mzr, me_v, mo_v, 0, 1)
    build(mp, mzr, me_v, mo_v, 9, 10)
    for i in range(3, 9):
        put(i, gsum[i - 3] + conv_grad(GROUPS[i], edge))
        if i == 5:
            s0(1).start()
        if i == 7:
            s0(2).start()
    for dx in (0, 2):
        where, d = back(dx, edge)
        acc[where] += d
    dz_of(0, 1)
    dz_of(7, 8)
    d = dsum[...] + dot(
        jnp.concatenate([patch_t[:, :128], patch_t[:, 896:]], axis=1),
        jnp.concatenate([dz_v[:128], dz_v[896:]], axis=0), 1, 0,
    )
    for i in range(4):
        grads[27 + i] = d[i * 128 : (i + 1) * 128].astype(BF)
    grads[31] = jnp.zeros((128, 128), BF)
    s0(3).start()
    s0_finish(1)
    s0_finish(2)
    s0_finish(3)

    d = dot(dz_v[...], wd_v[...].reshape(512, 128), 1, 1)
    for a in range(2):
        for b in range(2):
            i = 2 * a + b
            d_fine[:, a, :, b] = d[:, i * 128 : (i + 1) * 128].reshape(8, 16, 8, 128).astype(BF)

    s3_start(0)
    s3_start(1)

    landed(ah_r.at[0], far_bytes)
    landed(ah_r.at[1], near_bytes)
    build(ap, azr, ae_v, ao_v, 0, 10)
    for g in range(0, 9, 2):
        pair = [g, g + 1] if g < 8 else [8]
        left = jnp.concatenate([cut(ae_v, ao_v, h // 3, 8, h % 3) for h in pair], axis=1)
        right = wc_v[3 * g : 3 * g + 3 * len(pair)].reshape(384 * len(pair), 128)
        if g == 0:
            acc[...] = dot(left, right, 1, 0)
        else:
            acc[...] += dot(left, right, 1, 0)
    out[...] = (
        zv[...].astype(F32) + occ[None] * acc[...].reshape(8, 16, 8, 128)
    ).astype(BF)
    s4_start(0)
    s4_start(1)
    s4_finish(0)
    s4_finish(1)

    landed(halo_s, acc.at[0:568])
    landed(halo_s, acc.at[0:568])
    landed(s0_s, r0)
    landed(s1_s, r1.at[:, pl.ds(1, 15)])
    landed(s3_s, r3.at[:, pl.ds(1, 7)])
    landed(s4_s, r4.at[:, pl.ds(1, 7)])


def publish_kernel(*refs):
    ins, outs, sem = refs[:4], refs[4:8], refs[8]
    copies = [pltpu.make_async_copy(ins[i], outs[i], sem.at[i]) for i in range(4)]
    for c in copies:
        c.start()
    for c in copies:
        c.wait()


def publish(*arrays):
    return pl.pallas_call(
        publish_kernel,
        out_shape=tuple(jax.ShapeDtypeStruct(a.shape, a.dtype) for a in arrays),
        in_specs=[pl.BlockSpec(memory_space=pltpu.VMEM)] * 4,
        out_specs=(pl.BlockSpec(memory_space=pl.ANY),) * 4,
        scratch_shapes=[pltpu.SemaphoreType.DMA((4,))],
    )(*[pltpu.with_memory_space_constraint(a, pltpu.VMEM) for a in arrays])


def body(fine, occupied, w_down, w_conv, cotangent):
    fine = fine.reshape(8, 2, 16, 2, 8, 128)
    vm = pltpu.VMEM
    dma = pltpu.SemaphoreType.DMA
    scratch = [
        vm(fine.shape, BF), vm(w_down.shape, BF), vm(w_conv.shape, BF), vm(cotangent.shape, BF),
        vm((10, 18, 8, 128), BF), vm((10, 18, 8, 128), BF),
        vm((2, 8, 16, 1, 128), F32), vm((2, 8, 16, 1, 128), F32),
        vm((2, 10, 18, 1, 128), F32), vm((2, 10, 18, 1, 128), F32),
        vm((10, 144, 384), BF), vm((10, 128, 384), BF),
        vm((10, 144, 384), BF), vm((10, 128, 384), BF),
        vm((8, 16, 8, 128), BF),
        vm((128, 1024), BF), vm((512, 1024), BF),
        vm((1024, 128), F32), vm((1024, 128), BF),
        vm((32, 128, 128), BF),
        vm((4, 4, 128, 128), BF), vm((4, 4, 128, 128), BF),
        vm((4, 16, 32, 128), BF),
        vm((2, 4, 16, 128), BF), vm((2, 8, 16, 128), BF),
        vm((2, 16, 128), BF), vm((2, 8, 16, 128), BF),
        vm((6, 128, 384), F32), vm((512, 128), F32),
        pltpu.SMEM((1, 1, 2), jnp.int32),
        dma((5,)), dma, dma((2,)), dma((2,)),
        dma, dma((4,)), dma, dma((4,)), dma, dma((2,)), dma, dma((2,)),
    ]
    anym = pl.BlockSpec(memory_space=pl.ANY)
    vmem = pl.BlockSpec(memory_space=pltpu.VMEM)
    out, d_fine, d_wconv, d_wdown = pl.pallas_call(
        kernel,
        out_shape=(
            vm(cotangent.shape, BF), vm(fine.shape, BF),
            vm((27, 8, 128), F32), vm((4, 8, 128), F32),
        ),
        in_specs=[anym, anym, anym, anym, anym],
        out_specs=(vmem, vmem, vmem, vmem),
        scratch_shapes=scratch,
        compiler_params=pltpu.CompilerParams(
            collective_id=0, has_side_effects=True, vmem_limit_bytes=56 * 1024 * 1024
        ),
    )(fine, jnp.transpose(occupied, (0, 2, 1)), w_down, w_conv, cotangent)
    out, d_fine, d_wconv, d_wdown = publish(out, d_fine, d_wconv, d_wdown)
    return out, d_fine.reshape(16, 32, 8, 128), d_wconv, d_wdown


def solution(mesh):
    in_specs = (P("gx", "gy", "gz", None), P("gx", "gy", "gz"), P(), P(), P("gx", "gy", "gz", None))
    out_specs = (
        P("gx", "gy", "gz", None),
        P("gx", "gy", "gz", None),
        P(None, "gx", None),
        P(None, "gx", None),
    )
    return jax.shard_map(body, mesh=mesh, in_specs=in_specs, out_specs=out_specs, check_vma=False)
```

```python
import jax
import jax.numpy as jnp
from jax import lax
from jax.experimental import pallas as pl
from jax.experimental.pallas import tpu as pltpu
from jax.sharding import PartitionSpec as P

BF = jnp.bfloat16
F32 = jnp.float32
MESH = pl.DeviceIdType.MESH

NGX, NGY, NGZ = 16, 4, 4
NEIGHBOURS = [
    (sx, sy, sz)
    for sx in (0, -1, 1)
    for sz in (-1, 1, 0)
    for sy in (-1, 1, 0)
    if abs(sx) + abs(sy) + abs(sz) in (1, 2)
]
NEAR = 8
GROUPS = [3, 4, 5, 0, 1, 2, 6, 7, 8]
SLOTS = [3 * g + 2 - b for g in GROUPS for b in range(3)] + [27, 28, 29, 30]


def dot(a, b, ca, cb):
    return lax.dot_general(a, b, (((ca,), (cb,)), ((), ())), preferred_element_type=F32)


def kernel(
    fine, occupied, w_down, w_conv, cot,
    out, d_fine, d_wconv, d_wdown,
    fine_v, wd_v, wc_v, cot_v,
    mp, ap, mz, az, mze, aze, mzr, azr, mzer, azer, me_v, mo_v, ae_v, ao_v,
    zv, act_t, patch_t, acc, dz_v, grads,
    r0, p1, r1, p2, r3, p3, r4, gsum, dsum,
    occ_v, load_sem, halo_s, mh_r, ah_r, s0_s, s0_r, s1_s, s1_r, s3_s, s3_r, s4_s, s4_r,
):
    gx, gy, gz = lax.axis_index("gx"), lax.axis_index("gy"), lax.axis_index("gz")
    yy, zhi, xx = gx // 4, lax.rem(gx, 4), gy
    zlo, core = gz // 2, lax.rem(gz, 2)
    zz = zhi * 2 + zlo

    def near(s):
        return (
            lax.rem(gx + s[0] + NGX, NGX),
            lax.rem(gy + s[1] + NGY, NGY),
            lax.rem(gz + s[2] + NGZ, NGZ),
        )

    other = (gx, gy, gz + 1 - 2 * core)

    def plane(n):
        tx, ty = lax.rem(xx + lax.rem(n, 4), 4), lax.rem(yy + n // 4, 4)
        return tx, ty, (ty * 4 + zhi, tx, gz)

    def column(n):
        tz = lax.rem(zz + n, 8)
        return tz // 2, (yy * 4 + tz // 2, gy, lax.rem(tz, 2) * 2 + core)

    def row(n):
        tx, tc = lax.rem(xx + n // 2, 4), lax.rem(core + lax.rem(n, 2), 2)
        return (gx, tx, zlo * 2 + tc)

    loads = [
        pltpu.make_async_copy(a, b, load_sem.at[i])
        for i, (a, b) in enumerate(((cot, cot_v), (fine, fine_v), (w_down, wd_v), (w_conv, wc_v), (occupied, occ_v)))
    ]
    for c in loads:
        c.start()

    barrier = pltpu.get_barrier_semaphore()

    def greet(device):
        pl.semaphore_signal(barrier, inc=1, device_id=device, device_id_type=MESH)

    for s in NEIGHBOURS:
        greet(near(s))
    greet(other)

    @pl.loop(1, 16)
    def _(n):
        greet(plane(n)[2])

    @pl.loop(1, 8)
    def _(n):
        greet(column(n)[1])

    @pl.loop(1, 8)
    def _(n):
        greet(row(n))

    loads[4].wait()
    o0 = occ_v[0, 0, 0].astype(F32)
    o1 = occ_v[0, 0, 1].astype(F32)
    rows = lax.broadcasted_iota(jnp.int32, (16, 8, 128), 0)
    occ = jnp.where(rows < 8, o0, o1)
    loads[0].wait()

    @pl.loop(0, 8)
    def _(x):
        m = cot_v[x].astype(F32) * occ
        mp[x + 1, 1:17] = m.astype(BF)
        for side, k in ((0, 0), (1, 7)):
            mz[side, x] = m[:, k, :].astype(BF)
            mze[side, x, 0] = m[0, k : k + 1]
            mze[side, x, 1] = m[15, k : k + 1]

    pl.semaphore_wait(barrier, 18 + 1 + 15 + 7 + 7)

    def send(src, dst, sem, s):
        pltpu.make_async_remote_copy(
            src_ref=src, dst_ref=dst, send_sem=halo_s, recv_sem=sem,
            device_id=near(s), device_id_type=MESH,
        ).start()

    def halo(pad, zs, zse, zr, zer, rs):
        for i, (sx, sy, sz) in enumerate(NEIGHBOURS):
            sxs = {-1: slice(1, 2), 0: slice(1, 9), 1: slice(8, 9)}[sx]
            dxs = {-1: slice(9, 10), 0: slice(1, 9), 1: slice(0, 1)}[sx]
            sys_ = {-1: slice(1, 2), 0: slice(1, 17), 1: slice(16, 17)}[sy]
            dys = {-1: slice(17, 18), 0: slice(1, 17), 1: slice(0, 1)}[sy]
            up, down = (sz + 1) // 2, (1 - sz) // 2
            zxs = slice(sxs.start - 1, sxs.stop - 1)
            if sz == 0:
                src, dst = pad.at[sxs, sys_], pad.at[dxs, dys]
            elif sy == 0:
                src, dst = zs.at[up, zxs], zr.at[down, dxs]
            else:
                src = zse.at[up, zxs, (sy + 1) // 2]
                dst = zer.at[down, dxs, (1 - sy) // 2]
            send(src, dst, rs.at[1 if i < NEAR else 0], (sx, sy, sz))

    def corners(zer, rs):
        for sx in (-1, 1):
            for side in range(2):
                src = zer.at[side, 1 if sx < 0 else 8]
                dst = zer.at[side, 9 if sx < 0 else 0]
                send(src, dst, rs.at[0], (sx, 0, 0))

    def landed(sem, ref):
        pltpu.make_async_copy(ref, ref, sem).wait()

    far_bytes, near_bytes = acc.at[0:184], acc.at[0:224]

    halo(mp, mz, mze, mzr, mzer, mh_r)

    loads[1].wait()
    loads[2].wait()
    patches = [
        fine_v[:, a, :, b].reshape(1024, 128) for a in range(2) for b in range(2)
    ]
    z = dot(jnp.concatenate(patches, axis=1), wd_v[...].reshape(512, 128), 1, 0)
    zval = (z.reshape(8, 16, 8, 128) * occ[None]).astype(BF)
    act = jnp.maximum(zval.astype(F32), 0.0)
    zv[...] = zval
    ap[1:9, 1:17] = act.astype(BF)
    for side, k in ((0, 0), (1, 7)):
        az[side] = act[:, :, k, :].astype(BF)
        aze[side, :, 0] = act[:, 0, k : k + 1]
        aze[side, :, 1] = act[:, 15, k : k + 1]
    act_t[...] = act.reshape(1024, 128).T.astype(BF)
    for i in range(4):
        patch_t[i * 128 : (i + 1) * 128] = patches[i].T

    kk = lax.broadcasted_iota(jnp.int32, (18, 8, 128), 1)
    yi = lax.broadcasted_iota(jnp.int32, (18, 8, 128), 0)
    inside_y = jnp.logical_and(
        jnp.logical_or(yi > 0, gy > 0), jnp.logical_or(yi < 17, gy < NGY - 1)
    )

    def build(pad, zr, zer, even, odd, first, last):
        @pl.loop(first, last)
        def _(x):
            inside_x = jnp.logical_and(
                jnp.logical_or(x > 0, gx > 0), jnp.logical_or(x < 9, gx < NGX - 1)
            )
            keep = jnp.where(jnp.logical_and(inside_y, inside_x), 1.0, 0.0)
            low = jnp.where(gz > 0, 1.0, 0.0)
            high = jnp.where(gz < NGZ - 1, 1.0, 0.0)
            m = pad[x].astype(F32)
            face = [
                jnp.concatenate(
                    [zer[d, x, 0:1], zr[d, x].astype(F32)[:, None, :], zer[d, x, 1:2]], axis=0
                )
                for d in range(2)
            ]
            lo = jnp.where(kk == 0, face[0] * low, pltpu.roll(m, 1, 1)) * keep
            hi = jnp.where(kk == 7, face[1] * high, pltpu.roll(m, 7, 1)) * keep
            for b, v in enumerate((lo, m * keep, hi)):
                even[x, :, b * 128 : (b + 1) * 128] = v.reshape(144, 128).astype(BF)
                odd[x, :, b * 128 : (b + 1) * 128] = v[1:17].reshape(128, 128).astype(BF)

    def cut(even, odd, first, count, oy):
        if oy == 1:
            return odd[first : first + count].reshape(count * 128, 384)
        return even[first : first + count, oy * 8 : oy * 8 + 128].reshape(count * 128, 384)

    own = {0: (2, 0, 7), 1: (1, 0, 8), 2: (1, 1, 7)}
    edge = {0: (9, 7, 1), 2: (0, 0, 1)}

    def conv_grad(g, where):
        first, mine, count = where[g // 3]
        return dot(
            act_t[:, mine * 128 : (mine + count) * 128],
            cut(me_v, mo_v, first, count, 2 - g % 3), 1, 0,
        )

    def back(dx, where):
        first, mine, count = where[dx]
        left = jnp.concatenate(
            [cut(me_v, mo_v, first, count, 2 - dy) for dy in range(3)], axis=1
        )
        right = jnp.concatenate(
            [wc_v[9 * dx + 3 * dy + 2 - b] for dy in range(3) for b in range(3)], axis=1
        )
        return slice(mine * 128, (mine + count) * 128), dot(left, right, 1, 1)

    def back_own():
        left = jnp.concatenate([cut(me_v, mo_v, 1, 8, 2 - dy) for dy in range(3)], axis=1)
        right = [
            jnp.concatenate(
                [wc_v[9 * dx + 3 * dy + 2 - b] for dy in range(3) for b in range(3)], axis=1
            )
            for dx in range(3)
        ]
        both = dot(left, jnp.concatenate(right[:2], axis=0), 1, 1)
        acc[...] = both[:, 128:]
        acc[:896] += both[128:, :128]
        acc[128:] += dot(left[:896], right[2], 1, 1)

    def dz_of(first, last):
        d_act = acc[first * 128 : last * 128].reshape(last - first, 16, 8, 128)
        positive = zv[first:last].astype(F32) > 0
        dz = occ[None] * (cot_v[first:last].astype(F32) + jnp.where(positive, d_act, 0.0))
        dz_v[first * 128 : last * 128] = dz.reshape((last - first) * 128, 128).astype(BF)

    def s0(j):
        return pltpu.make_async_remote_copy(
            src_ref=grads.at[pl.ds(8 * j + 4 - 4 * core, 4)], dst_ref=r0.at[j],
            send_sem=s0_s, recv_sem=s0_r.at[j], device_id=other, device_id_type=MESH,
        )

    def s1(j, n):
        tx, ty, device = plane(n)
        return pltpu.make_async_remote_copy(
            src_ref=p1.at[j, tx, pl.ds(pl.multiple_of(ty * 32, 32), 32)], dst_ref=r1.at[j, n],
            send_sem=s1_s, recv_sem=s1_r.at[j],
            device_id=device, device_id_type=MESH,
        )

    def s0_finish(j):
        s0(j).wait_recv()
        p1[j] = (grads[pl.ds(8 * j + 4 * core, 4)].astype(F32) + r0[j].astype(F32)).astype(BF)

        @pl.loop(1, 16)
        def _(n):
            s1(j, n).start()

    def s1_finish(j):
        landed(s1_r.at[j], r1.at[j, pl.ds(1, 15)])

        total = p1[j, xx, pl.ds(pl.multiple_of(yy * 32, 32), 32)].astype(F32)
        for n in range(1, 16):
            total = total + r1[j, n].astype(F32)
        return total

    def s3(i, n):
        h, device = column(n)
        return pltpu.make_async_remote_copy(
            src_ref=p2.at[i, h], dst_ref=r3.at[i, n],
            send_sem=s3_s, recv_sem=s3_r.at[i],
            device_id=device, device_id_type=MESH,
        )

    def s4(i, n):
        return pltpu.make_async_remote_copy(
            src_ref=p3.at[i], dst_ref=r4.at[i, xx * 2 + core],
            send_sem=s4_s, recv_sem=s4_r.at[i],
            device_id=row(n), device_id_type=MESH,
        )

    def s3_start(i):
        low, high = s1_finish(2 * i), s1_finish(2 * i + 1)
        for h in range(4):
            p2[i, h] = jnp.concatenate(
                [low[h * 8 : h * 8 + 8], high[h * 8 : h * 8 + 8]], axis=0
            ).astype(BF)

        @pl.loop(1, 8)
        def _(n):
            s3(i, n).start()

    def s4_start(i):
        landed(s3_r.at[i], r3.at[i, pl.ds(1, 7)])

        total = p2[i, zhi].astype(F32)
        for n in range(1, 8):
            total = total + r3[i, n].astype(F32)
        mine = total.astype(BF)
        p3[i] = mine
        r4[i, xx * 2 + core] = mine

        @pl.loop(1, 8)
        def _(n):
            s4(i, n).start()

    def s4_finish(i):
        landed(s4_r.at[i], r4.at[i, pl.ds(1, 7)])

        for x in range(4):
            for c in range(2):
                v = r4[i, x * 2 + c].astype(F32) * (262144.0 ** -0.5)
                for h in range(2):
                    slot = 8 * (2 * i + h) + 4 * c + x
                    if slot == 31:
                        continue
                    tap = SLOTS[slot]
                    if tap < 27:
                        d_wconv[tap] = v[8 * h : 8 * h + 8]
                    else:
                        d_wdown[tap - 27] = v[8 * h : 8 * h + 8]

    def put(i, d):
        for b in range(3):
            grads[3 * i + b] = d[:, b * 128 : (b + 1) * 128].astype(BF)

    landed(mh_r.at[1], near_bytes)
    corners(mzer, mh_r)
    halo(ap, az, aze, azr, azer, ah_r)
    build(mp, mzr, mzer, me_v, mo_v, 1, 9)
    for i in range(3):
        put(i, conv_grad(GROUPS[i], own))
    s0(0).start()
    loads[3].wait()
    s0_finish(0)
    for i in range(3, 9):
        gsum[i - 3] = conv_grad(GROUPS[i], own)

    landed(mh_r.at[0], far_bytes)
    build(mp, mzr, mzer, me_v, mo_v, 0, 1)
    build(mp, mzr, mzer, me_v, mo_v, 9, 10)
    for i in range(3, 9):
        put(i, gsum[i - 3] + conv_grad(GROUPS[i], edge))
        if i == 5:
            s0(1).start()
        if i == 7:
            s0(2).start()
    back_own()
    for dx in (0, 2):
        where, d = back(dx, edge)
        acc[where] += d
    dz_of(0, 8)
    s0_finish(1)
    d = dot(patch_t[...], dz_v[...], 1, 0)
    for i in range(4):
        grads[27 + i] = d[i * 128 : (i + 1) * 128].astype(BF)
    grads[31] = jnp.zeros((128, 128), BF)
    s0(3).start()
    s0_finish(2)
    s0_finish(3)
    landed(ah_r.at[1], near_bytes)
    corners(azer, ah_r)

    d = dot(dz_v[...], wd_v[...].reshape(512, 128), 1, 1)
    for a in range(2):
        for b in range(2):
            i = 2 * a + b
            d_fine[:, a, :, b] = d[:, i * 128 : (i + 1) * 128].reshape(8, 16, 8, 128).astype(BF)

    s3_start(0)
    s3_start(1)

    landed(ah_r.at[0], far_bytes)
    build(ap, azr, azer, ae_v, ao_v, 0, 10)
    for g in range(0, 9, 2):
        pair = [g, g + 1] if g < 8 else [8]
        left = jnp.concatenate([cut(ae_v, ao_v, h // 3, 8, h % 3) for h in pair], axis=1)
        right = wc_v[3 * g : 3 * g + 3 * len(pair)].reshape(384 * len(pair), 128)
        if g == 0:
            acc[...] = dot(left, right, 1, 0)
        else:
            acc[...] += dot(left, right, 1, 0)
    out[...] = (
        zv[...].astype(F32) + occ[None] * acc[...].reshape(8, 16, 8, 128)
    ).astype(BF)
    s4_start(0)
    s4_start(1)
    s4_finish(0)
    s4_finish(1)

    landed(halo_s, acc.at[0:408])
    landed(halo_s, acc.at[0:408])
    landed(s0_s, r0)
    landed(s1_s, r1.at[:, pl.ds(1, 15)])
    landed(s3_s, r3.at[:, pl.ds(1, 7)])
    landed(s4_s, r4.at[:, pl.ds(1, 7)])


def publish_kernel(*refs):
    ins, outs, sem = refs[:4], refs[4:8], refs[8]
    copies = [pltpu.make_async_copy(ins[i], outs[i], sem.at[i]) for i in range(4)]
    for c in copies:
        c.start()
    for c in copies:
        c.wait()


def publish(*arrays):
    return pl.pallas_call(
        publish_kernel,
        out_shape=tuple(jax.ShapeDtypeStruct(a.shape, a.dtype) for a in arrays),
        in_specs=[pl.BlockSpec(memory_space=pltpu.VMEM)] * 4,
        out_specs=(pl.BlockSpec(memory_space=pl.ANY),) * 4,
        scratch_shapes=[pltpu.SemaphoreType.DMA((4,))],
    )(*[pltpu.with_memory_space_constraint(a, pltpu.VMEM) for a in arrays])


def body(fine, occupied, w_down, w_conv, cotangent):
    fine = fine.reshape(8, 2, 16, 2, 8, 128)
    vm = pltpu.VMEM
    dma = pltpu.SemaphoreType.DMA
    scratch = [
        vm(fine.shape, BF), vm(w_down.shape, BF), vm(w_conv.shape, BF), vm(cotangent.shape, BF),
        vm((10, 18, 8, 128), BF), vm((10, 18, 8, 128), BF),
        vm((2, 8, 16, 128), BF), vm((2, 8, 16, 128), BF),
        vm((2, 8, 2, 1, 128), F32), vm((2, 8, 2, 1, 128), F32),
        vm((2, 10, 16, 128), BF), vm((2, 10, 16, 128), BF),
        vm((2, 10, 2, 1, 128), F32), vm((2, 10, 2, 1, 128), F32),
        vm((10, 144, 384), BF), vm((10, 128, 384), BF),
        vm((10, 144, 384), BF), vm((10, 128, 384), BF),
        vm((8, 16, 8, 128), BF),
        vm((128, 1024), BF), vm((512, 1024), BF),
        vm((1024, 128), F32), vm((1024, 128), BF),
        vm((32, 128, 128), BF),
        vm((4, 4, 128, 128), BF), vm((4, 4, 128, 128), BF),
        vm((4, 16, 32, 128), BF),
        vm((2, 4, 16, 128), BF), vm((2, 8, 16, 128), BF),
        vm((2, 16, 128), BF), vm((2, 8, 16, 128), BF),
        vm((6, 128, 384), F32), vm((512, 128), F32),
        pltpu.SMEM((1, 1, 2), jnp.int32),
        dma((5,)), dma, dma((2,)), dma((2,)),
        dma, dma((4,)), dma, dma((4,)), dma, dma((2,)), dma, dma((2,)),
    ]
    anym = pl.BlockSpec(memory_space=pl.ANY)
    vmem = pl.BlockSpec(memory_space=pltpu.VMEM)
    out, d_fine, d_wconv, d_wdown = pl.pallas_call(
        kernel,
        out_shape=(
            vm(cotangent.shape, BF), vm(fine.shape, BF),
            vm((27, 8, 128), F32), vm((4, 8, 128), F32),
        ),
        in_specs=[anym, anym, anym, anym, anym],
        out_specs=(vmem, vmem, vmem, vmem),
        scratch_shapes=scratch,
        compiler_params=pltpu.CompilerParams(
            collective_id=0, has_side_effects=True, vmem_limit_bytes=56 * 1024 * 1024
        ),
    )(fine, jnp.transpose(occupied, (0, 2, 1)), w_down, w_conv, cotangent)
    out, d_fine, d_wconv, d_wdown = publish(out, d_fine, d_wconv, d_wdown)
    return out, d_fine.reshape(16, 32, 8, 128), d_wconv, d_wdown


def solution(mesh):
    in_specs = (P("gx", "gy", "gz", None), P("gx", "gy", "gz"), P(), P(), P("gx", "gy", "gz", None))
    out_specs = (
        P("gx", "gy", "gz", None),
        P("gx", "gy", "gz", None),
        P(None, "gx", None),
        P(None, "gx", None),
    )
    return jax.shard_map(body, mesh=mesh, in_specs=in_specs, out_specs=out_specs, check_vma=False)
```

```python
import jax
import jax.numpy as jnp
from jax import lax
from jax.experimental import pallas as pl
from jax.experimental.pallas import tpu as pltpu
from jax.sharding import PartitionSpec as P

BF = jnp.bfloat16
F32 = jnp.float32
MESH = pl.DeviceIdType.MESH
REST = [(dy, b) for dy in range(3) for b in range(3) if (dy, b) != (1, 1)]

NGX, NGY, NGZ = 16, 4, 4
NEIGHBOURS = [
    (sx, sy, sz)
    for sx in (0, -1, 1)
    for sz in (-1, 1, 0)
    for sy in (-1, 1, 0)
    if abs(sx) + abs(sy) + abs(sz) in (1, 2)
]
NEAR = 8
GROUPS = [3, 4, 5, 0, 1, 2, 6, 7, 8]
SLOTS = [3 * g + 2 - b for g in GROUPS for b in range(3)] + [27, 28, 29, 30]


def dot(a, b, ca, cb):
    return lax.dot_general(a, b, (((ca,), (cb,)), ((), ())), preferred_element_type=F32)


def kernel(
    fine, occupied, w_down, w_conv, cot,
    out, d_fine, d_wconv, d_wdown,
    fine_v, wd_v, wc_v, cot_v,
    mp, ap, mz, az, mze, aze, mzr, azr, mzer, azer, me_v, mo_v, ae_v, ao_v,
    zv, act_t, patch_t, acc, dz_v, grads,
    r0, p1, r1, p2, r3, p3, r4, gsum, centre,
    occ_v, load_sem, halo_s, mh_r, ah_r, s0_s, s0_r, s1_s, s1_r, s3_s, s3_r, s4_s, s4_r,
):
    gx, gy, gz = lax.axis_index("gx"), lax.axis_index("gy"), lax.axis_index("gz")
    yy, zhi, xx = gx // 4, lax.rem(gx, 4), gy
    zlo, core = gz // 2, lax.rem(gz, 2)
    zz = zhi * 2 + zlo

    def near(s):
        return (
            lax.rem(gx + s[0] + NGX, NGX),
            lax.rem(gy + s[1] + NGY, NGY),
            lax.rem(gz + s[2] + NGZ, NGZ),
        )

    other = (gx, gy, gz + 1 - 2 * core)

    def plane(n):
        tx, ty = lax.rem(xx + lax.rem(n, 4), 4), lax.rem(yy + n // 4, 4)
        return tx, ty, (ty * 4 + zhi, tx, gz)

    def column(n):
        tz = lax.rem(zz + n, 8)
        return tz // 2, (yy * 4 + tz // 2, gy, lax.rem(tz, 2) * 2 + core)

    def row(n):
        tx, tc = lax.rem(xx + n // 2, 4), lax.rem(core + lax.rem(n, 2), 2)
        return (gx, tx, zlo * 2 + tc)

    loads = [
        pltpu.make_async_copy(a, b, load_sem.at[i])
        for i, (a, b) in enumerate(((cot, cot_v), (fine, fine_v), (w_down, wd_v), (w_conv, wc_v), (occupied, occ_v)))
    ]
    for c in loads:
        c.start()

    barrier = pltpu.get_barrier_semaphore()

    def greet(device):
        pl.semaphore_signal(barrier, inc=1, device_id=device, device_id_type=MESH)

    for s in NEIGHBOURS:
        greet(near(s))
    greet(other)

    @pl.loop(1, 16)
    def _(n):
        greet(plane(n)[2])

    @pl.loop(1, 8)
    def _(n):
        greet(column(n)[1])

    @pl.loop(1, 8)
    def _(n):
        greet(row(n))

    loads[4].wait()
    o0 = occ_v[0, 0, 0].astype(F32)
    o1 = occ_v[0, 0, 1].astype(F32)
    rows = lax.broadcasted_iota(jnp.int32, (16, 8, 128), 0)
    occ = jnp.where(rows < 8, o0, o1)
    loads[0].wait()

    @pl.loop(0, 8)
    def _(x):
        m = cot_v[x].astype(F32) * occ
        mp[x + 1, 1:17] = m.astype(BF)
        for side, k in ((0, 0), (1, 7)):
            mz[side, x] = m[:, k, :].astype(BF)
            mze[side, x, 0] = m[0, k : k + 1]
            mze[side, x, 1] = m[15, k : k + 1]

    pl.semaphore_wait(barrier, 18 + 1 + 15 + 7 + 7)

    def send(src, dst, sem, s):
        pltpu.make_async_remote_copy(
            src_ref=src, dst_ref=dst, send_sem=halo_s, recv_sem=sem,
            device_id=near(s), device_id_type=MESH,
        ).start()

    def halo(pad, zs, zse, zr, zer, rs):
        for i, (sx, sy, sz) in enumerate(NEIGHBOURS):
            sxs = {-1: slice(1, 2), 0: slice(1, 9), 1: slice(8, 9)}[sx]
            dxs = {-1: slice(9, 10), 0: slice(1, 9), 1: slice(0, 1)}[sx]
            sys_ = {-1: slice(1, 2), 0: slice(1, 17), 1: slice(16, 17)}[sy]
            dys = {-1: slice(17, 18), 0: slice(1, 17), 1: slice(0, 1)}[sy]
            up, down = (sz + 1) // 2, (1 - sz) // 2
            zxs = slice(sxs.start - 1, sxs.stop - 1)
            if sz == 0:
                src, dst = pad.at[sxs, sys_], pad.at[dxs, dys]
            elif sy == 0:
                src, dst = zs.at[up, zxs], zr.at[down, dxs]
            else:
                src = zse.at[up, zxs, (sy + 1) // 2]
                dst = zer.at[down, dxs, (1 - sy) // 2]
            send(src, dst, rs.at[1 if i < NEAR else 0], (sx, sy, sz))

    def corners(zer, rs):
        for sx in (-1, 1):
            for side in range(2):
                src = zer.at[side, 1 if sx < 0 else 8]
                dst = zer.at[side, 9 if sx < 0 else 0]
                send(src, dst, rs.at[0], (sx, 0, 0))

    def landed(sem, ref):
        pltpu.make_async_copy(ref, ref, sem).wait()

    far_bytes, near_bytes = acc.at[0:184], acc.at[0:224]

    halo(mp, mz, mze, mzr, mzer, mh_r)

    loads[1].wait()
    loads[2].wait()
    patches = [
        fine_v[:, a, :, b].reshape(1024, 128) for a in range(2) for b in range(2)
    ]
    z = dot(jnp.concatenate(patches, axis=1), wd_v[...].reshape(512, 128), 1, 0)
    zval = (z.reshape(8, 16, 8, 128) * occ[None]).astype(BF)
    act = jnp.maximum(zval.astype(F32), 0.0)
    zv[...] = zval
    ap[1:9, 1:17] = act.astype(BF)
    for side, k in ((0, 0), (1, 7)):
        az[side] = act[:, :, k, :].astype(BF)
        aze[side, :, 0] = act[:, 0, k : k + 1]
        aze[side, :, 1] = act[:, 15, k : k + 1]
    act_t[...] = act.reshape(1024, 128).T.astype(BF)
    for i in range(4):
        patch_t[i * 128 : (i + 1) * 128] = patches[i].T

    kk = lax.broadcasted_iota(jnp.int32, (18, 8, 128), 1)
    yi = lax.broadcasted_iota(jnp.int32, (18, 8, 128), 0)
    inside_y = jnp.logical_and(
        jnp.logical_or(yi > 0, gy > 0), jnp.logical_or(yi < 17, gy < NGY - 1)
    )

    def build(pad, zr, zer, even, odd, first, last):
        @pl.loop(first, last)
        def _(x):
            inside_x = jnp.logical_and(
                jnp.logical_or(x > 0, gx > 0), jnp.logical_or(x < 9, gx < NGX - 1)
            )
            keep = jnp.where(jnp.logical_and(inside_y, inside_x), 1.0, 0.0)
            low = jnp.where(gz > 0, 1.0, 0.0)
            high = jnp.where(gz < NGZ - 1, 1.0, 0.0)
            m = pad[x].astype(F32)
            face = [
                jnp.concatenate(
                    [zer[d, x, 0:1], zr[d, x].astype(F32)[:, None, :], zer[d, x, 1:2]], axis=0
                )
                for d in range(2)
            ]
            lo = jnp.where(kk == 0, face[0] * low, pltpu.roll(m, 1, 1)) * keep
            hi = jnp.where(kk == 7, face[1] * high, pltpu.roll(m, 7, 1)) * keep
            for b, v in enumerate((lo, m * keep, hi)):
                even[x, :, b * 128 : (b + 1) * 128] = v.reshape(144, 128).astype(BF)
                odd[x, :, b * 128 : (b + 1) * 128] = v[1:17].reshape(128, 128).astype(BF)

    def cut(even, odd, first, count, oy):
        if oy == 1:
            return odd[first : first + count].reshape(count * 128, 384)
        return even[first : first + count, oy * 8 : oy * 8 + 128].reshape(count * 128, 384)

    own = {0: (2, 0, 7), 1: (1, 0, 8), 2: (1, 1, 7)}
    edge = {0: (9, 7, 1), 2: (0, 0, 1)}

    def conv_grad(dx, where):
        first, mine, count = where[dx]
        if where is own:
            right = rest(first, count)
        else:
            right = [cut(me_v, mo_v, first, count, 2 - dy) for dy in range(3)]
        return dot(
            act_t[:, mine * 128 : (mine + count) * 128], jnp.concatenate(right, axis=1), 1, 0
        )

    def back(dx, where):
        first, mine, count = where[dx]
        left = jnp.concatenate(
            [cut(me_v, mo_v, first, count, 2 - dy) for dy in range(3)], axis=1
        )
        right = jnp.concatenate(
            [wc_v[9 * dx + 3 * dy + 2 - b] for dy in range(3) for b in range(3)], axis=1
        )
        return slice(mine * 128, (mine + count) * 128), dot(left, right, 1, 1)

    def rest(first, count):
        return [
            cut(me_v, mo_v, first, count, 2),
            mo_v[first : first + count, :, :128].reshape(count * 128, 128),
            mo_v[first : first + count, :, 256:].reshape(count * 128, 128),
            cut(me_v, mo_v, first, count, 0),
        ]

    def back_own():
        left = jnp.concatenate(rest(1, 8), axis=1)
        right = [
            jnp.concatenate([wc_v[9 * dx + 3 * dy + 2 - b] for dy, b in REST], axis=1)
            for dx in range(3)
        ]
        both = dot(left, jnp.concatenate(right[:2], axis=0), 1, 1)
        acc[...] += both[:, 128:]
        acc[:896] += both[128:, :128]
        acc[128:] += dot(left[:896], right[2], 1, 1)

    def dz_of(first, last):
        d_act = acc[first * 128 : last * 128].reshape(last - first, 16, 8, 128)
        positive = zv[first:last].astype(F32) > 0
        dz = occ[None] * (cot_v[first:last].astype(F32) + jnp.where(positive, d_act, 0.0))
        dz_v[first * 128 : last * 128] = dz.reshape((last - first) * 128, 128).astype(BF)

    def s0(j):
        return pltpu.make_async_remote_copy(
            src_ref=grads.at[pl.ds(8 * j + 4 - 4 * core, 4)], dst_ref=r0.at[j],
            send_sem=s0_s, recv_sem=s0_r.at[j], device_id=other, device_id_type=MESH,
        )

    def s1(j, n):
        tx, ty, device = plane(n)
        return pltpu.make_async_remote_copy(
            src_ref=p1.at[j, tx, pl.ds(pl.multiple_of(ty * 32, 32), 32)], dst_ref=r1.at[j, n],
            send_sem=s1_s, recv_sem=s1_r.at[j],
            device_id=device, device_id_type=MESH,
        )

    def s0_finish(j):
        s0(j).wait_recv()
        p1[j] = (grads[pl.ds(8 * j + 4 * core, 4)].astype(F32) + r0[j].astype(F32)).astype(BF)

        @pl.loop(1, 16)
        def _(n):
            s1(j, n).start()

    def s1_finish(j):
        landed(s1_r.at[j], r1.at[j, pl.ds(1, 15)])

        total = p1[j, xx, pl.ds(pl.multiple_of(yy * 32, 32), 32)].astype(F32)
        for n in range(1, 16):
            total = total + r1[j, n].astype(F32)
        return total

    def s3(i, n):
        h, device = column(n)
        return pltpu.make_async_remote_copy(
            src_ref=p2.at[i, h], dst_ref=r3.at[i, n],
            send_sem=s3_s, recv_sem=s3_r.at[i],
            device_id=device, device_id_type=MESH,
        )

    def s4(i, n):
        return pltpu.make_async_remote_copy(
            src_ref=p3.at[i], dst_ref=r4.at[i, xx * 2 + core],
            send_sem=s4_s, recv_sem=s4_r.at[i],
            device_id=row(n), device_id_type=MESH,
        )

    def s3_start(i):
        low, high = s1_finish(2 * i), s1_finish(2 * i + 1)
        for h in range(4):
            p2[i, h] = jnp.concatenate(
                [low[h * 8 : h * 8 + 8], high[h * 8 : h * 8 + 8]], axis=0
            ).astype(BF)

        @pl.loop(1, 8)
        def _(n):
            s3(i, n).start()

    def s4_start(i):
        landed(s3_r.at[i], r3.at[i, pl.ds(1, 7)])

        total = p2[i, zhi].astype(F32)
        for n in range(1, 8):
            total = total + r3[i, n].astype(F32)
        mine = total.astype(BF)
        p3[i] = mine
        r4[i, xx * 2 + core] = mine

        @pl.loop(1, 8)
        def _(n):
            s4(i, n).start()

    def s4_finish(i):
        landed(s4_r.at[i], r4.at[i, pl.ds(1, 7)])

        for x in range(4):
            for c in range(2):
                v = r4[i, x * 2 + c].astype(F32) * (262144.0 ** -0.5)
                for h in range(2):
                    slot = 8 * (2 * i + h) + 4 * c + x
                    if slot == 31:
                        continue
                    tap = SLOTS[slot]
                    if tap < 27:
                        d_wconv[tap] = v[8 * h : 8 * h + 8]
                    else:
                        d_wdown[tap - 27] = v[8 * h : 8 * h + 8]

    def put(i, d, middle=None):
        parts = [d[:, b : b + 128] for b in range(0, d.shape[1], 128)]
        if middle is not None:
            parts.insert(4, middle)
        for b in range(9):
            grads[9 * i + b] = parts[b].astype(BF)

    loads[3].wait()
    local = mp[1:9, 1:17].reshape(1024, 128)
    both = dot(local, jnp.concatenate([wc_v[4], wc_v[13]], axis=0), 1, 1)
    acc[...] = both[:, 128:]
    acc[:896] += both[128:, :128]
    acc[128:] += dot(local[:896], wc_v[22], 1, 1)
    centre[0] = dot(act_t[:, :896], local[128:], 1, 0)
    centre[1] = dot(act_t[...], local, 1, 0)
    centre[2] = dot(act_t[:, 128:], local[:896], 1, 0)

    landed(mh_r.at[1], near_bytes)
    corners(mzer, mh_r)
    halo(ap, az, aze, azr, azer, ah_r)
    build(mp, mzr, mzer, me_v, mo_v, 1, 9)
    put(0, conv_grad(1, own), centre[1])
    s0(0).start()
    for i, dx in enumerate((0, 2)):
        d = conv_grad(dx, own)
        gsum[i, :, :512] = d[:, :512]
        gsum[i, :, 512:640] = centre[dx]
        gsum[i, :, 640:] = d[:, 512:]

    s0_finish(0)
    back_own()

    landed(mh_r.at[0], far_bytes)
    build(mp, mzr, mzer, me_v, mo_v, 0, 1)
    build(mp, mzr, mzer, me_v, mo_v, 9, 10)
    put(1, gsum[0] + conv_grad(0, edge))
    s0(1).start()
    put(2, gsum[1] + conv_grad(2, edge))
    s0(2).start()
    for dx in (0, 2):
        where, d = back(dx, edge)
        acc[where] += d
    dz_of(0, 8)
    s0_finish(1)
    d = dot(patch_t[...], dz_v[...], 1, 0)
    for i in range(4):
        grads[27 + i] = d[i * 128 : (i + 1) * 128].astype(BF)
    grads[31] = jnp.zeros((128, 128), BF)
    s0(3).start()
    s0_finish(2)
    s0_finish(3)
    landed(ah_r.at[1], near_bytes)
    corners(azer, ah_r)

    d = dot(dz_v[...], wd_v[...].reshape(512, 128), 1, 1)
    for a in range(2):
        for b in range(2):
            i = 2 * a + b
            d_fine[:, a, :, b] = d[:, i * 128 : (i + 1) * 128].reshape(8, 16, 8, 128).astype(BF)

    s3_start(0)
    s3_start(1)

    landed(ah_r.at[0], far_bytes)
    build(ap, azr, azer, ae_v, ao_v, 0, 10)
    for g in range(0, 9, 2):
        pair = [g, g + 1] if g < 8 else [8]
        left = jnp.concatenate([cut(ae_v, ao_v, h // 3, 8, h % 3) for h in pair], axis=1)
        right = wc_v[3 * g : 3 * g + 3 * len(pair)].reshape(384 * len(pair), 128)
        if g == 0:
            acc[...] = dot(left, right, 1, 0)
        else:
            acc[...] += dot(left, right, 1, 0)
    out[...] = (
        zv[...].astype(F32) + occ[None] * acc[...].reshape(8, 16, 8, 128)
    ).astype(BF)
    s4_start(0)
    s4_start(1)
    s4_finish(0)
    s4_finish(1)

    landed(halo_s, acc.at[0:408])
    landed(halo_s, acc.at[0:408])
    landed(s0_s, r0)
    landed(s1_s, r1.at[:, pl.ds(1, 15)])
    landed(s3_s, r3.at[:, pl.ds(1, 7)])
    landed(s4_s, r4.at[:, pl.ds(1, 7)])


def publish_kernel(*refs):
    ins, outs, sem = refs[:4], refs[4:8], refs[8]
    copies = [pltpu.make_async_copy(ins[i], outs[i], sem.at[i]) for i in range(4)]
    for c in copies:
        c.start()
    for c in copies:
        c.wait()


def publish(*arrays):
    return pl.pallas_call(
        publish_kernel,
        out_shape=tuple(jax.ShapeDtypeStruct(a.shape, a.dtype) for a in arrays),
        in_specs=[pl.BlockSpec(memory_space=pltpu.VMEM)] * 4,
        out_specs=(pl.BlockSpec(memory_space=pl.ANY),) * 4,
        scratch_shapes=[pltpu.SemaphoreType.DMA((4,))],
    )(*[pltpu.with_memory_space_constraint(a, pltpu.VMEM) for a in arrays])


def body(fine, occupied, w_down, w_conv, cotangent):
    fine = fine.reshape(8, 2, 16, 2, 8, 128)
    vm = pltpu.VMEM
    dma = pltpu.SemaphoreType.DMA
    scratch = [
        vm(fine.shape, BF), vm(w_down.shape, BF), vm(w_conv.shape, BF), vm(cotangent.shape, BF),
        vm((10, 18, 8, 128), BF), vm((10, 18, 8, 128), BF),
        vm((2, 8, 16, 128), BF), vm((2, 8, 16, 128), BF),
        vm((2, 8, 2, 1, 128), F32), vm((2, 8, 2, 1, 128), F32),
        vm((2, 10, 16, 128), BF), vm((2, 10, 16, 128), BF),
        vm((2, 10, 2, 1, 128), F32), vm((2, 10, 2, 1, 128), F32),
        vm((10, 144, 384), BF), vm((10, 128, 384), BF),
        vm((10, 144, 384), BF), vm((10, 128, 384), BF),
        vm((8, 16, 8, 128), BF),
        vm((128, 1024), BF), vm((512, 1024), BF),
        vm((1024, 128), F32), vm((1024, 128), BF),
        vm((32, 128, 128), BF),
        vm((4, 4, 128, 128), BF), vm((4, 4, 128, 128), BF),
        vm((4, 16, 32, 128), BF),
        vm((2, 4, 16, 128), BF), vm((2, 8, 16, 128), BF),
        vm((2, 16, 128), BF), vm((2, 8, 16, 128), BF),
        vm((2, 128, 1152), F32), vm((3, 128, 128), F32),
        pltpu.SMEM((1, 1, 2), jnp.int32),
        dma((5,)), dma, dma((2,)), dma((2,)),
        dma, dma((4,)), dma, dma((4,)), dma, dma((2,)), dma, dma((2,)),
    ]
    anym = pl.BlockSpec(memory_space=pl.ANY)
    vmem = pl.BlockSpec(memory_space=pltpu.VMEM)
    out, d_fine, d_wconv, d_wdown = pl.pallas_call(
        kernel,
        out_shape=(
            vm(cotangent.shape, BF), vm(fine.shape, BF),
            vm((27, 8, 128), F32), vm((4, 8, 128), F32),
        ),
        in_specs=[anym, anym, anym, anym, anym],
        out_specs=(vmem, vmem, vmem, vmem),
        scratch_shapes=scratch,
        compiler_params=pltpu.CompilerParams(
            collective_id=0, has_side_effects=True, vmem_limit_bytes=56 * 1024 * 1024
        ),
    )(fine, jnp.transpose(occupied, (0, 2, 1)), w_down, w_conv, cotangent)
    out, d_fine, d_wconv, d_wdown = publish(out, d_fine, d_wconv, d_wdown)
    return out, d_fine.reshape(16, 32, 8, 128), d_wconv, d_wdown


def solution(mesh):
    in_specs = (P("gx", "gy", "gz", None), P("gx", "gy", "gz"), P(), P(), P("gx", "gy", "gz", None))
    out_specs = (
        P("gx", "gy", "gz", None),
        P("gx", "gy", "gz", None),
        P(None, "gx", None),
        P(None, "gx", None),
    )
    return jax.shard_map(body, mesh=mesh, in_specs=in_specs, out_specs=out_specs, check_vma=False)
```

```python
import jax
import jax.numpy as jnp
from jax import lax
from jax.experimental import pallas as pl
from jax.experimental.pallas import tpu as pltpu
from jax.sharding import PartitionSpec as P

BF = jnp.bfloat16
F32 = jnp.float32
MESH = pl.DeviceIdType.MESH
REST = [(dy, b) for dy in range(3) for b in range(3) if (dy, b) != (1, 1)]

NGX, NGY, NGZ = 16, 4, 4
NEIGHBOURS = [
    (sx, sy, sz)
    for sx in (0, -1, 1)
    for sz in (-1, 1, 0)
    for sy in (-1, 1, 0)
    if abs(sx) + abs(sy) + abs(sz) in (1, 2)
]
NEAR = 8
GROUPS = [3, 4, 5, 0, 1, 2, 6, 7, 8]
SLOTS = [3 * g + 2 - b for g in GROUPS for b in range(3)] + [27, 28, 29, 30]


def dot(a, b, ca, cb):
    return lax.dot_general(a, b, (((ca,), (cb,)), ((), ())), preferred_element_type=F32)


def kernel(
    fine, occupied, w_down, w_conv, cot,
    out, d_fine, d_wconv, d_wdown,
    fine_v, wd_v, wc_v, cot_v,
    mp, ap, mz, az, mze, aze, mzr, azr, mzer, azer, me_v, mo_v, ae_v, ao_v,
    zv, act_t, patch_t, acc, dz_v, grads,
    r0, p1, r1, p2, r3, p3, r4, gsum, centre,
    occ_v, load_sem, halo_s, mh_r, ah_r, s0_s, s0_r, s1_s, s1_r, s3_s, s3_r, s4_s, s4_r,
):
    gx, gy, gz = lax.axis_index("gx"), lax.axis_index("gy"), lax.axis_index("gz")
    yy, zhi, xx = gx // 4, lax.rem(gx, 4), gy
    zlo, core = gz // 2, lax.rem(gz, 2)
    zz = zhi * 2 + zlo

    def near(s):
        return (
            lax.rem(gx + s[0] + NGX, NGX),
            lax.rem(gy + s[1] + NGY, NGY),
            lax.rem(gz + s[2] + NGZ, NGZ),
        )

    other = (gx, gy, gz + 1 - 2 * core)

    def plane(n):
        tx, ty = lax.rem(xx + lax.rem(n, 4), 4), lax.rem(yy + n // 4, 4)
        return tx, ty, (ty * 4 + zhi, tx, gz)

    def column(n):
        tz = lax.rem(zz + n, 8)
        return tz // 2, (yy * 4 + tz // 2, gy, lax.rem(tz, 2) * 2 + core)

    def row(n):
        tx, tc = lax.rem(xx + n // 2, 4), lax.rem(core + lax.rem(n, 2), 2)
        return (gx, tx, zlo * 2 + tc)

    loads = [
        pltpu.make_async_copy(a, b, load_sem.at[i])
        for i, (a, b) in enumerate(((cot, cot_v), (fine, fine_v), (w_down, wd_v), (w_conv, wc_v), (occupied, occ_v)))
    ]
    for c in loads:
        c.start()

    barrier = pltpu.get_barrier_semaphore()

    def greet(device):
        pl.semaphore_signal(barrier, inc=1, device_id=device, device_id_type=MESH)

    for s in NEIGHBOURS:
        greet(near(s))
    greet(other)

    @pl.loop(1, 16)
    def _(n):
        greet(plane(n)[2])

    @pl.loop(1, 8)
    def _(n):
        greet(column(n)[1])

    @pl.loop(1, 8)
    def _(n):
        greet(row(n))

    loads[4].wait()
    o0 = occ_v[0, 0, 0].astype(F32)
    o1 = occ_v[0, 0, 1].astype(F32)
    rows = lax.broadcasted_iota(jnp.int32, (16, 8, 128), 0)
    occ = jnp.where(rows < 8, o0, o1)
    loads[0].wait()

    @pl.loop(0, 8)
    def _(x):
        m = cot_v[x].astype(F32) * occ
        mp[x + 1, 1:17] = m.astype(BF)
        for side, k in ((0, 0), (1, 7)):
            mz[side, x] = m[:, k, :].astype(BF)
            mze[side, x, 0] = m[0, k : k + 1]
            mze[side, x, 1] = m[15, k : k + 1]

    pl.semaphore_wait(barrier, 18 + 1 + 15 + 7 + 7)

    def send(src, dst, sem, s):
        pltpu.make_async_remote_copy(
            src_ref=src, dst_ref=dst, send_sem=halo_s, recv_sem=sem,
            device_id=near(s), device_id_type=MESH,
        ).start()

    def halo(pad, zs, zse, zr, zer, rs):
        for i, (sx, sy, sz) in enumerate(NEIGHBOURS):
            sxs = {-1: slice(1, 2), 0: slice(1, 9), 1: slice(8, 9)}[sx]
            dxs = {-1: slice(9, 10), 0: slice(1, 9), 1: slice(0, 1)}[sx]
            sys_ = {-1: slice(1, 2), 0: slice(1, 17), 1: slice(16, 17)}[sy]
            dys = {-1: slice(17, 18), 0: slice(1, 17), 1: slice(0, 1)}[sy]
            up, down = (sz + 1) // 2, (1 - sz) // 2
            zxs = slice(sxs.start - 1, sxs.stop - 1)
            if sz == 0:
                src, dst = pad.at[sxs, sys_], pad.at[dxs, dys]
            elif sy == 0:
                src, dst = zs.at[up, zxs], zr.at[down, dxs]
            else:
                src = zse.at[up, zxs, (sy + 1) // 2]
                dst = zer.at[down, dxs, (1 - sy) // 2]
            send(src, dst, rs.at[1 if i < NEAR else 0], (sx, sy, sz))

    def corners(zer, rs):
        for sx in (-1, 1):
            for side in range(2):
                src = zer.at[side, 1 if sx < 0 else 8]
                dst = zer.at[side, 9 if sx < 0 else 0]
                send(src, dst, rs.at[0], (sx, 0, 0))

    def landed(sem, ref):
        pltpu.make_async_copy(ref, ref, sem).wait()

    far_bytes, near_bytes = acc.at[0:184], acc.at[0:224]

    halo(mp, mz, mze, mzr, mzer, mh_r)

    loads[1].wait()
    loads[2].wait()
    patches = [
        fine_v[:, a, :, b].reshape(1024, 128) for a in range(2) for b in range(2)
    ]
    z = dot(jnp.concatenate(patches, axis=1), wd_v[...].reshape(512, 128), 1, 0)
    zval = (z.reshape(8, 16, 8, 128) * occ[None]).astype(BF)
    act = jnp.maximum(zval.astype(F32), 0.0)
    zv[...] = zval
    ap[1:9, 1:17] = act.astype(BF)
    for side, k in ((0, 0), (1, 7)):
        az[side] = act[:, :, k, :].astype(BF)
        aze[side, :, 0] = act[:, 0, k : k + 1]
        aze[side, :, 1] = act[:, 15, k : k + 1]
    act_t[...] = act.reshape(1024, 128).T.astype(BF)
    for i in range(4):
        patch_t[i * 128 : (i + 1) * 128] = patches[i].T

    kk = lax.broadcasted_iota(jnp.int32, (18, 8, 128), 1)
    yi = lax.broadcasted_iota(jnp.int32, (18, 8, 128), 0)
    inside_y = jnp.logical_and(
        jnp.logical_or(yi > 0, gy > 0), jnp.logical_or(yi < 17, gy < NGY - 1)
    )

    def build(pad, zr, zer, even, odd, first, last):
        @pl.loop(first, last)
        def _(x):
            inside_x = jnp.logical_and(
                jnp.logical_or(x > 0, gx > 0), jnp.logical_or(x < 9, gx < NGX - 1)
            )
            keep = jnp.where(jnp.logical_and(inside_y, inside_x), 1.0, 0.0)
            low = jnp.where(gz > 0, 1.0, 0.0)
            high = jnp.where(gz < NGZ - 1, 1.0, 0.0)
            m = pad[x].astype(F32)
            face = [
                jnp.concatenate(
                    [zer[d, x, 0:1], zr[d, x].astype(F32)[:, None, :], zer[d, x, 1:2]], axis=0
                )
                for d in range(2)
            ]
            lo = jnp.where(kk == 0, face[0] * low, pltpu.roll(m, 1, 1)) * keep
            hi = jnp.where(kk == 7, face[1] * high, pltpu.roll(m, 7, 1)) * keep
            for b, v in enumerate((lo, m * keep, hi)):
                even[x, :, b * 128 : (b + 1) * 128] = v.reshape(144, 128).astype(BF)
                odd[x, :, b * 128 : (b + 1) * 128] = v[1:17].reshape(128, 128).astype(BF)

    def cut(even, odd, first, count, oy):
        if oy == 1:
            return odd[first : first + count].reshape(count * 128, 384)
        return even[first : first + count, oy * 8 : oy * 8 + 128].reshape(count * 128, 384)

    own = {0: (2, 0, 7), 1: (1, 0, 8), 2: (1, 1, 7)}
    edge = {0: (9, 7, 1), 2: (0, 0, 1)}

    def conv_grad(dx, where):
        first, mine, count = where[dx]
        if where is own:
            right = rest(first, count)
        else:
            right = [cut(me_v, mo_v, first, count, 2 - dy) for dy in range(3)]
        return dot(
            act_t[:, mine * 128 : (mine + count) * 128], jnp.concatenate(right, axis=1), 1, 0
        )

    def back(dx, where):
        first, mine, count = where[dx]
        left = jnp.concatenate(
            [cut(me_v, mo_v, first, count, 2 - dy) for dy in range(3)], axis=1
        )
        right = jnp.concatenate(
            [wc_v[9 * dx + 3 * dy + 2 - b] for dy in range(3) for b in range(3)], axis=1
        )
        return slice(mine * 128, (mine + count) * 128), dot(left, right, 1, 1)

    def rest(first, count):
        return [
            cut(me_v, mo_v, first, count, 2),
            mo_v[first : first + count, :, :128].reshape(count * 128, 128),
            mo_v[first : first + count, :, 256:].reshape(count * 128, 128),
            cut(me_v, mo_v, first, count, 0),
        ]

    def back_own():
        left = jnp.concatenate(rest(1, 8), axis=1)
        right = [
            jnp.concatenate([wc_v[9 * dx + 3 * dy + 2 - b] for dy, b in REST], axis=1)
            for dx in range(3)
        ]
        both = dot(left, jnp.concatenate(right[:2], axis=0), 1, 1)
        acc[...] += both[:, 128:]
        acc[:896] += both[128:, :128]
        acc[128:] += dot(left[:896], right[2], 1, 1)

    def dz_of(first, last):
        d_act = acc[first * 128 : last * 128].reshape(last - first, 16, 8, 128)
        positive = zv[first:last].astype(F32) > 0
        dz = occ[None] * (cot_v[first:last].astype(F32) + jnp.where(positive, d_act, 0.0))
        dz_v[first * 128 : last * 128] = dz.reshape((last - first) * 128, 128).astype(BF)

    def s0(j):
        return pltpu.make_async_remote_copy(
            src_ref=grads.at[pl.ds(8 * j + 4 - 4 * core, 4)], dst_ref=r0.at[j],
            send_sem=s0_s, recv_sem=s0_r.at[j], device_id=other, device_id_type=MESH,
        )

    def s1(j, n):
        tx, ty, device = plane(n)
        return pltpu.make_async_remote_copy(
            src_ref=p1.at[j, tx, pl.ds(pl.multiple_of(ty * 32, 32), 32)], dst_ref=r1.at[j, n],
            send_sem=s1_s, recv_sem=s1_r.at[j],
            device_id=device, device_id_type=MESH,
        )

    def s0_finish(j):
        s0(j).wait_recv()
        p1[j] = (grads[pl.ds(8 * j + 4 * core, 4)].astype(F32) + r0[j].astype(F32)).astype(BF)

        @pl.loop(1, 16)
        def _(n):
            s1(j, lax.rem(n + 8, 15) + 1).start()

    def s1_finish(j):
        landed(s1_r.at[j], r1.at[j, pl.ds(1, 15)])

        total = p1[j, xx, pl.ds(pl.multiple_of(yy * 32, 32), 32)].astype(F32)
        for n in range(1, 16):
            total = total + r1[j, n].astype(F32)
        return total

    def s3(i, n):
        h, device = column(n)
        return pltpu.make_async_remote_copy(
            src_ref=p2.at[i, h], dst_ref=r3.at[i, n],
            send_sem=s3_s, recv_sem=s3_r.at[i],
            device_id=device, device_id_type=MESH,
        )

    def s4(i, n):
        return pltpu.make_async_remote_copy(
            src_ref=p3.at[i], dst_ref=r4.at[i, xx * 2 + core],
            send_sem=s4_s, recv_sem=s4_r.at[i],
            device_id=row(n), device_id_type=MESH,
        )

    def s3_start(i):
        low, high = s1_finish(2 * i), s1_finish(2 * i + 1)
        for h in range(4):
            p2[i, h] = jnp.concatenate(
                [low[h * 8 : h * 8 + 8], high[h * 8 : h * 8 + 8]], axis=0
            ).astype(BF)

        @pl.loop(1, 8)
        def _(n):
            s3(i, n).start()

    def s4_start(i):
        landed(s3_r.at[i], r3.at[i, pl.ds(1, 7)])

        total = p2[i, zhi].astype(F32)
        for n in range(1, 8):
            total = total + r3[i, n].astype(F32)
        mine = total.astype(BF)
        p3[i] = mine
        r4[i, xx * 2 + core] = mine

        @pl.loop(1, 8)
        def _(n):
            s4(i, n).start()

    def s4_finish(i):
        landed(s4_r.at[i], r4.at[i, pl.ds(1, 7)])

        for x in range(4):
            for c in range(2):
                v = r4[i, x * 2 + c].astype(F32) * (262144.0 ** -0.5)
                for h in range(2):
                    slot = 8 * (2 * i + h) + 4 * c + x
                    if slot == 31:
                        continue
                    tap = SLOTS[slot]
                    if tap < 27:
                        d_wconv[tap] = v[8 * h : 8 * h + 8]
                    else:
                        d_wdown[tap - 27] = v[8 * h : 8 * h + 8]

    def put(i, d, middle=None):
        parts = [d[:, b : b + 128] for b in range(0, d.shape[1], 128)]
        if middle is not None:
            parts.insert(4, middle)
        for b in range(9):
            grads[9 * i + b] = parts[b].astype(BF)

    loads[3].wait()
    local = mp[1:9, 1:17].reshape(1024, 128)
    both = dot(local, jnp.concatenate([wc_v[4], wc_v[13]], axis=0), 1, 1)
    acc[...] = both[:, 128:]
    acc[:896] += both[128:, :128]
    acc[128:] += dot(local[:896], wc_v[22], 1, 1)
    centre[0] = dot(act_t[:, :896], local[128:], 1, 0)
    centre[1] = dot(act_t[...], local, 1, 0)
    centre[2] = dot(act_t[:, 128:], local[:896], 1, 0)

    landed(mh_r.at[1], near_bytes)
    corners(mzer, mh_r)
    halo(ap, az, aze, azr, azer, ah_r)
    build(mp, mzr, mzer, me_v, mo_v, 1, 9)
    put(0, conv_grad(1, own), centre[1])
    s0(0).start()
    for i, dx in enumerate((0, 2)):
        d = conv_grad(dx, own)
        gsum[i, :, :512] = d[:, :512]
        gsum[i, :, 512:640] = centre[dx]
        gsum[i, :, 640:] = d[:, 512:]

    s0_finish(0)
    back_own()

    landed(mh_r.at[0], far_bytes)
    build(mp, mzr, mzer, me_v, mo_v, 0, 1)
    build(mp, mzr, mzer, me_v, mo_v, 9, 10)
    put(1, gsum[0] + conv_grad(0, edge))
    s0(1).start()
    put(2, gsum[1] + conv_grad(2, edge))
    s0(2).start()
    for dx in (0, 2):
        where, d = back(dx, edge)
        acc[where] += d
    dz_of(0, 8)
    s0_finish(1)
    d = dot(patch_t[...], dz_v[...], 1, 0)
    for i in range(4):
        grads[27 + i] = d[i * 128 : (i + 1) * 128].astype(BF)
    grads[31] = jnp.zeros((128, 128), BF)
    s0(3).start()
    s0_finish(2)
    s0_finish(3)
    landed(ah_r.at[1], near_bytes)
    corners(azer, ah_r)

    d = dot(dz_v[...], wd_v[...].reshape(512, 128), 1, 1)
    for a in range(2):
        for b in range(2):
            i = 2 * a + b
            d_fine[:, a, :, b] = d[:, i * 128 : (i + 1) * 128].reshape(8, 16, 8, 128).astype(BF)

    s3_start(0)
    s3_start(1)

    landed(ah_r.at[0], far_bytes)
    build(ap, azr, azer, ae_v, ao_v, 0, 10)
    for g in range(0, 9, 2):
        pair = [g, g + 1] if g < 8 else [8]
        left = jnp.concatenate([cut(ae_v, ao_v, h // 3, 8, h % 3) for h in pair], axis=1)
        right = wc_v[3 * g : 3 * g + 3 * len(pair)].reshape(384 * len(pair), 128)
        if g == 0:
            acc[...] = dot(left, right, 1, 0)
        else:
            acc[...] += dot(left, right, 1, 0)
    out[...] = (
        zv[...].astype(F32) + occ[None] * acc[...].reshape(8, 16, 8, 128)
    ).astype(BF)
    s4_start(0)
    s4_start(1)
    s4_finish(0)
    s4_finish(1)

    landed(halo_s, acc.at[0:408])
    landed(halo_s, acc.at[0:408])
    landed(s0_s, r0)
    landed(s1_s, r1.at[:, pl.ds(1, 15)])
    landed(s3_s, r3.at[:, pl.ds(1, 7)])
    landed(s4_s, r4.at[:, pl.ds(1, 7)])


def publish_kernel(*refs):
    ins, outs, sem = refs[:4], refs[4:8], refs[8]
    copies = [pltpu.make_async_copy(ins[i], outs[i], sem.at[i]) for i in range(4)]
    for c in copies:
        c.start()
    for c in copies:
        c.wait()


def publish(*arrays):
    return pl.pallas_call(
        publish_kernel,
        out_shape=tuple(jax.ShapeDtypeStruct(a.shape, a.dtype) for a in arrays),
        in_specs=[pl.BlockSpec(memory_space=pltpu.VMEM)] * 4,
        out_specs=(pl.BlockSpec(memory_space=pl.ANY),) * 4,
        scratch_shapes=[pltpu.SemaphoreType.DMA((4,))],
    )(*[pltpu.with_memory_space_constraint(a, pltpu.VMEM) for a in arrays])


def body(fine, occupied, w_down, w_conv, cotangent):
    fine = fine.reshape(8, 2, 16, 2, 8, 128)
    vm = pltpu.VMEM
    dma = pltpu.SemaphoreType.DMA
    scratch = [
        vm(fine.shape, BF), vm(w_down.shape, BF), vm(w_conv.shape, BF), vm(cotangent.shape, BF),
        vm((10, 18, 8, 128), BF), vm((10, 18, 8, 128), BF),
        vm((2, 8, 16, 128), BF), vm((2, 8, 16, 128), BF),
        vm((2, 8, 2, 1, 128), F32), vm((2, 8, 2, 1, 128), F32),
        vm((2, 10, 16, 128), BF), vm((2, 10, 16, 128), BF),
        vm((2, 10, 2, 1, 128), F32), vm((2, 10, 2, 1, 128), F32),
        vm((10, 144, 384), BF), vm((10, 128, 384), BF),
        vm((10, 144, 384), BF), vm((10, 128, 384), BF),
        vm((8, 16, 8, 128), BF),
        vm((128, 1024), BF), vm((512, 1024), BF),
        vm((1024, 128), F32), vm((1024, 128), BF),
        vm((32, 128, 128), BF),
        vm((4, 4, 128, 128), BF), vm((4, 4, 128, 128), BF),
        vm((4, 16, 32, 128), BF),
        vm((2, 4, 16, 128), BF), vm((2, 8, 16, 128), BF),
        vm((2, 16, 128), BF), vm((2, 8, 16, 128), BF),
        vm((2, 128, 1152), F32), vm((3, 128, 128), F32),
        pltpu.SMEM((1, 1, 2), jnp.int32),
        dma((5,)), dma, dma((2,)), dma((2,)),
        dma, dma((4,)), dma, dma((4,)), dma, dma((2,)), dma, dma((2,)),
    ]
    anym = pl.BlockSpec(memory_space=pl.ANY)
    vmem = pl.BlockSpec(memory_space=pltpu.VMEM)
    out, d_fine, d_wconv, d_wdown = pl.pallas_call(
        kernel,
        out_shape=(
            vm(cotangent.shape, BF), vm(fine.shape, BF),
            vm((27, 8, 128), F32), vm((4, 8, 128), F32),
        ),
        in_specs=[anym, anym, anym, anym, anym],
        out_specs=(vmem, vmem, vmem, vmem),
        scratch_shapes=scratch,
        compiler_params=pltpu.CompilerParams(
            collective_id=0, has_side_effects=True, vmem_limit_bytes=56 * 1024 * 1024
        ),
    )(fine, jnp.transpose(occupied, (0, 2, 1)), w_down, w_conv, cotangent)
    out, d_fine, d_wconv, d_wdown = publish(out, d_fine, d_wconv, d_wdown)
    return out, d_fine.reshape(16, 32, 8, 128), d_wconv, d_wdown


def solution(mesh):
    in_specs = (P("gx", "gy", "gz", None), P("gx", "gy", "gz"), P(), P(), P("gx", "gy", "gz", None))
    out_specs = (
        P("gx", "gy", "gz", None),
        P("gx", "gy", "gz", None),
        P(None, "gx", None),
        P(None, "gx", None),
    )
    return jax.shard_map(body, mesh=mesh, in_specs=in_specs, out_specs=out_specs, check_vma=False)
```
